512 devices in a mesh: wave: 64 (over y, z), lev: 8 (over x, core).
Axes of the slice: x: 4, y: 8, z: 8, core: 2. Of those that a mesh axis runs over, the one named last changes fastest.
Arguments:
- spectral: bfloat16 [820480, 1024], P('wave', 'lev'), may hold values from -0.1796875 to 0.1796875
- table: bfloat16 [32, 820480], P('lev', 'wave'), may hold values from -0.15625 to 0.15625
- wave_owner: int32 [1280], replicated, may hold values from 0 to 63, as said below
- lat_owner: int32 [64], replicated, may hold values from 0 to 63, as said below
- lat_points: int32 [32], replicated, may hold values from 20 to 5136, as said below
Outputs:
- grid: bfloat16 [64, 512, 5376], P('wave', 'lev')
The draws below stay inside these ranges and needn't reach their ends.
Inputs may be any that keep to these rules, and one draw needn't show every extreme that they name: `wave_owner`: wavenumbers m and 1279 - m have the same owner, and every index of wave owns exactly 10 such pairs. `lat_owner`: every index of wave owns exactly one latitude. `lat_points`: values 20 + 4 i for distinct latitude rows i from 0 to 1279, both ends among them.
All inputs are finite; a program needn't handle non-finite values.
Results may differ from the reference program's by a relative error of at most 0.0055.
Values may be sent and summed in bfloat16 or wider, within the bound.
No kernel may reach another device: no remote copies, remote signals or barrier semaphores. Data moves between devices by JAX's collectives and lax.ppermute only.
A program may use at most 128 MiB of HBM per device.

```python
import math
import jax
import jax.numpy as jnp
from jax import lax

TRUNC = 1279
WAVES = 1280
PAIRS_DEV = 10
PAIR_ROWS = 1282
ROWS = 820480
LF = 512
NLAT = 64
NLAT_N = 32
NLON_PAD = 5376
N_WAVE = 64


def draw_wave_owner(key, part):
    key = jax.random.fold_in(key, 1)
    pair_count = (TRUNC + 1) // 2
    shuffled = jax.random.permutation(key, pair_count).astype(jnp.int32)
    owners = shuffled // PAIRS_DEV
    return jnp.concatenate([owners, owners[::-1]]).astype(jnp.int32)


def draw_lat_owner(key, part):
    key = jax.random.fold_in(key, 2)
    return jax.random.permutation(key, NLAT).astype(jnp.int32)


def draw_lat_points(key, part):
    key = jax.random.fold_in(key, 3)
    first_key, second_key = jax.random.split(key)
    inner = jax.random.permutation(first_key, TRUNC - 1)[:NLAT_N - 2].astype(jnp.int32) + 1
    chosen = jnp.concatenate([jnp.array([0, TRUNC], jnp.int32), inner])
    chosen = jax.random.permutation(second_key, chosen)
    return (20 + 4 * chosen).astype(jnp.int32)


def steps_of(stream_key, shape, cuts, smallest, top_value):
    factor_of, own = 1.0, jax.random.fold_in(stream_key, 6)
    for axis_at, parts in cuts:
        steps = jnp.exp(jax.random.uniform(jax.random.fold_in(own, axis_at), (parts,), jnp.float32, smallest / len(cuts), top_value / len(cuts)))
        factor_of = factor_of * jnp.repeat(steps, shape[axis_at] // parts).reshape([-1 if axis == axis_at else 1 for axis in range(len(shape))])
    return factor_of


def centred(rng, shape, spread, most, cuts=(), kind=jnp.bfloat16):
    level = steps_of(rng, shape, cuts, -0.22, 0.18) if cuts else 1.0
    drawn = jax.random.normal(rng, shape, jnp.float32) * spread * level
    return jnp.minimum(jnp.maximum(drawn, -most), most).astype(kind)


def setup_inputs(seed: int = 0) -> dict:
    splits = jax.random.split(jax.random.key(seed), 6)
    spectral = centred(splits[0], (ROWS, 2 * LF), 0.03, 0.1796875, ((0, 64), (1, 8)))
    table = centred(splits[1], (NLAT_N, ROWS), WAVES ** -0.5, 0.15625, ((0, 8), (1, 64)))
    wave_owner = draw_wave_owner(jax.random.fold_in(splits[5], 71), 0)
    lat_owner = draw_lat_owner(jax.random.fold_in(splits[5], 71), 0)
    lat_points = draw_lat_points(jax.random.fold_in(splits[5], 71), 0)
    return dict(spectral=spectral, table=table, wave_owner=wave_owner, lat_owner=lat_owner, lat_points=lat_points)


block_width = 896
wave_block = 128


def pair_slots(wave_owner, device_count, pairs_per_device):
    pair_count = wave_owner.shape[0] // 2
    owners = wave_owner[:pair_count]
    onehot = (owners[:, None] == jnp.arange(device_count, dtype=jnp.int32)[None, :]).astype(jnp.int32)
    earlier = jnp.cumsum(onehot, axis=0) - onehot
    position = jnp.sum(earlier * onehot, axis=1).astype(jnp.int32)
    global_slot = (owners * pairs_per_device + position).astype(jnp.int32)
    return jnp.zeros((pair_count,), jnp.int32).at[global_slot].set(jnp.arange(pair_count, dtype=jnp.int32))


def legendre_slot(arguments):
    pair_index, rows_block, table_block = arguments
    row_index = jnp.arange(PAIR_ROWS, dtype=jnp.int32)
    split_row = TRUNC + 1 - pair_index
    low_mask = row_index < split_row
    high_mask = jnp.logical_and(row_index >= split_row, row_index < TRUNC + 2)
    zero_value = jnp.zeros((), rows_block.dtype)
    low_part = jnp.where(low_mask[:, None], rows_block, zero_value)
    high_part = jnp.where(high_mask[:, None], rows_block, zero_value)
    low_sign = (1 - 2 * (row_index % 2)).astype(rows_block.dtype)
    high_sign = (1 - 2 * ((row_index + pair_index) % 2)).astype(rows_block.dtype)
    table_wide = table_block.astype(jnp.float32)
    outputs = []
    for part, sign in ((low_part, low_sign), (high_part, high_sign)):
        north = jnp.dot(table_wide, part.astype(jnp.float32), precision=lax.Precision.HIGHEST)
        south = jnp.dot(table_wide, (part * sign[:, None]).astype(jnp.float32), precision=lax.Precision.HIGHEST)
        outputs.append(jnp.concatenate([north, south], axis=0))
    return jnp.stack(outputs, axis=0)


def reference(spectral, table, wave_owner, lat_owner, lat_points):
    slot_count = N_WAVE * PAIRS_DEV
    columns = 2 * LF
    pair_of_slot = pair_slots(wave_owner, N_WAVE, PAIRS_DEV)
    rows_blocks = spectral.reshape(slot_count, PAIR_ROWS, columns)
    table_blocks = jnp.transpose(table.reshape(NLAT_N, slot_count, PAIR_ROWS), (1, 0, 2))
    four = lax.map(legendre_slot, (pair_of_slot, rows_blocks, table_blocks))
    four = four.astype(jnp.bfloat16).reshape(WAVES, NLAT, columns)
    wave_index = jnp.stack([pair_of_slot, TRUNC - pair_of_slot], axis=1).reshape(WAVES).astype(jnp.int32)
    by_wave = jnp.zeros((NLAT, WAVES, columns), jnp.bfloat16).at[:, wave_index].set(jnp.transpose(four, (1, 0, 2)))
    holder = jnp.zeros((NLAT,), jnp.int32).at[lat_owner].set(jnp.arange(NLAT, dtype=jnp.int32))

    def one_device(device):
        latitude = holder[device]
        points = lat_points[latitude % NLAT_N]
        rows_wide = by_wave[latitude].astype(jnp.float32).reshape(WAVES, LF, 2)
        used_waves = jnp.minimum(WAVES, (points + 1) // 2)
        wave_steps = (used_waves + wave_block - 1) // wave_block

        def column_block(index, grid_rows):
            first = index * block_width
            col_index = first + jnp.arange(block_width, dtype=jnp.int32)
            valid = (col_index < points)[None, :]

            def wave_step(step_index, total):
                wave_first = step_index * wave_block
                wave_numbers = wave_first + jnp.arange(wave_block, dtype=jnp.int32)
                part = lax.dynamic_slice_in_dim(rows_wide, wave_first, wave_block, 0)
                weights = jnp.where(wave_numbers == 0, 1.0, 2.0) * (2 * wave_numbers < points)
                weights = weights.astype(jnp.float32)
                phase = (wave_numbers[:, None] * col_index[None, :]) % points
                angle = (2.0 * math.pi) * phase.astype(jnp.float32) / points.astype(jnp.float32)
                cosine = jnp.where(valid, weights[:, None] * jnp.cos(angle), 0.0)
                sine = jnp.where(valid, -weights[:, None] * jnp.sin(angle), 0.0)
                basis = jnp.stack([cosine, sine], axis=0).astype(jnp.bfloat16).astype(jnp.float32)
                return total + jnp.einsum('mlc,cmj->lj', part, basis, precision=lax.Precision.HIGHEST)

            values = lax.fori_loop(0, wave_steps, wave_step, jnp.zeros((LF, block_width), jnp.float32))
            return lax.dynamic_update_slice_in_dim(grid_rows, values, first, 1)

        block_count = (points + block_width - 1) // block_width
        grid_rows = lax.fori_loop(0, block_count, column_block, jnp.zeros((LF, NLON_PAD), jnp.float32))
        return grid_rows.astype(jnp.bfloat16)

    return lax.map(one_device, jnp.arange(N_WAVE, dtype=jnp.int32))
```

```python
import functools
import math

import jax
import jax.numpy as jnp
from jax import lax
from jax.experimental import pallas as pl
from jax.experimental.pallas import tpu as pltpu
from jax.sharding import PartitionSpec as P

TRUNC = 1279
PAIRS = 640
PAIRS_DEV = 10
PAIR_ROWS = 1282
ROWS_DEV = 12820
ROWS_PAD = 12928
N_WAVE = 64
NLAT = 64
NORTH = 32
LEVELS = 64
COLS = 128
SLOTS = 20
QUARTER = 1408
NLON_PAD = 5376
LANE = 128

VMEM = pl.BlockSpec(memory_space=pltpu.VMEM)
SMEM = pl.BlockSpec(memory_space=pltpu.SMEM)
f32 = jnp.float32
bf16 = jnp.bfloat16


def iota(shape, dim):
    return lax.broadcasted_iota(jnp.int32, shape, dim)


def to_column(row):
    eye = iota((LANE, LANE), 0) == iota((LANE, LANE), 1)
    parts = []
    for first in range(0, row.shape[1], LANE):
        block = jnp.broadcast_to(row[:, first : first + LANE], (LANE, LANE))
        parts.append(jnp.sum(jnp.where(eye, block, 0.0), axis=1, keepdims=True))
    return jnp.concatenate(parts, axis=0)


def slot_pairs(owner_row):
    owner_col = to_column(owner_row)
    pair_row = iota((1, PAIRS), 1)
    rank = jnp.zeros((1, PAIRS), f32)
    for first in range(0, PAIRS, LANE):
        same = owner_col[first : first + LANE] == owner_row
        earlier = (iota((LANE, PAIRS), 0) + first) < pair_row
        rank += jnp.sum(jnp.where(same & earlier, 1.0, 0.0), axis=0, keepdims=True)
    slot_col = to_column(rank * N_WAVE + owner_row)
    slot_row = iota((1, PAIRS), 1).astype(f32)
    pairs = jnp.zeros((1, PAIRS), f32)
    for first in range(0, PAIRS, LANE):
        here = slot_col[first : first + LANE] == slot_row
        pair = (iota((LANE, PAIRS), 0) + first).astype(f32)
        pairs += jnp.sum(jnp.where(here, pair, 0.0), axis=0, keepdims=True)
    return pairs


def is_odd(value):
    return value - 2.0 * jnp.floor(value * 0.5)


def slots_kernel(me_ref, owner_ref, pairs_ref, local_ref):
    pairs = slot_pairs(owner_ref[...].astype(f32))
    pairs_ref[...] = jnp.broadcast_to(pairs, (8, PAIRS))
    own = iota((16, PAIRS), 0) * N_WAVE + me_ref[0] == iota((16, PAIRS), 1)
    local = jnp.sum(jnp.where(own, pairs, 0.0), axis=1, keepdims=True)
    local_ref[...] = jnp.broadcast_to(local, (16, LANE))


def legendre_kernel(lat_owner_ref, local_ref, table_ref, spectral_ref, out_ref, table, four):
    for index in range(8):
        table[4 * index : 4 * index + 4, 0:ROWS_DEV] = table_ref[index].astype(f32)
    for pair in range(PAIRS_DEV):
        start = PAIR_ROWS * pair // LANE * LANE
        stop = min(-(-PAIR_ROWS * (pair + 1) // LANE) * LANE, ROWS_DEV)
        width = stop - start
        row = (iota((1, width), 1) + (start - PAIR_ROWS * pair)).astype(f32)
        q = local_ref[pair : pair + 1, 0:1]
        q_odd = is_odd(q)
        split = TRUNC + 1 - q
        low = jnp.where((row >= 0) & (row < split), 1.0, 0.0)
        high = jnp.where((row >= split) & (row < TRUNC + 2), 1.0, 0.0)
        even = jnp.where(q_odd > 0, high, low)
        odd = low + high - even
        odd_sign = 1.0 - 2.0 * is_odd(row)
        even_sign = odd_sign * (1.0 - 2.0 * q_odd)
        block = table[:, start:stop]
        left = jnp.concatenate(
            [block * even, block * (even * even_sign), block * odd, block * (odd * odd_sign)], axis=0
        ).astype(bf16)
        values = jnp.dot(left, spectral_ref[start:stop, :], preferred_element_type=f32)
        four[pair * NLAT : (pair + 1) * NLAT, :] = values[:NLAT]
        four[(PAIRS_DEV + pair) * NLAT : (PAIRS_DEV + pair + 1) * NLAT, :] = values[NLAT:]
    for latitude in range(NLAT):
        owner = lat_owner_ref[latitude]
        for part in range(SLOTS // 4):
            rows = four[pl.ds(4 * part * NLAT + latitude, 4, stride=NLAT), :]
            out_ref[owner, part] = rows.astype(bf16)


def circle(quarters_per_turn, numerator, inverse):
    turns = jnp.floor(numerator * inverse + 0.5)
    v = (numerator - turns * quarters_per_turn) * inverse
    z = v * v
    h = math.pi / 2
    sine = v * (h + z * (-(h**3) / 6 + z * (h**5 / 120 + z * (-(h**7) / 5040))))
    cosine = 1.0 + z * (-(h**2) / 2 + z * (h**4 / 24 + z * (-(h**6) / 720 + z * (h**8 / 40320))))
    halves = jnp.floor(turns * 0.5)
    odd_turn = turns - 2.0 * halves
    flip = 1.0 - 2.0 * is_odd(halves)
    swap = odd_turn > 0.5
    out_cos = jnp.where(swap, sine, cosine) * (flip * (1.0 - 2.0 * odd_turn))
    out_sin = jnp.where(swap, cosine, sine) * flip
    return out_cos, -out_sin


def my_points(me_ref, lat_owner_ref, lat_points_ref):
    latitude = jnp.int32(0)
    for index in range(NLAT):
        latitude = jnp.where(lat_owner_ref[index] == me_ref[0], index % NORTH, latitude)
    return lat_points_ref[latitude]


def basis_kernel(me_ref, lat_owner_ref, lat_points_ref, pairs_ref, after_ref, basis_ref, scale_ref, waves):
    del after_ref
    points = my_points(me_ref, lat_owner_ref, lat_points_ref)
    pair = pairs_ref[0:1, :]
    even = jnp.where(is_odd(pair) > 0, TRUNC - pair, pair)
    for index, wave in enumerate((even, TRUNC - even)):
        weight = jnp.where(wave == 0, 1.0, 2.0) * jnp.where(2.0 * wave < points.astype(f32), 1.0, 0.0)
        sign = 1.0 - 2.0 * is_odd(jnp.floor(wave * 0.5))
        scale_ref[2 * index : 2 * index + 1, :] = weight
        scale_ref[2 * index + 1 : 2 * index + 2, :] = weight * sign
        waves[index * PAIRS : (index + 1) * PAIRS, :] = jnp.broadcast_to(to_column(wave), (PAIRS, LANE))
    scale_ref[4:8, :] = jnp.zeros((4, PAIRS), f32)
    quarter = jnp.full((1, LANE), (points // 4).astype(f32))
    inverse = 1.0 / quarter
    step = 32
    column = iota((step, LANE), 1).astype(f32)

    for index in range(2):

        def rows_of(block, carry):
            first = pl.multiple_of(block * step, step)
            wave = waves[pl.ds(index * PAIRS + first, step), :]
            cosine, sine = circle(quarter, wave * column, inverse)
            turn_cos, turn_sin = circle(quarter, wave * float(LANE), inverse)
            for tile in range(QUARTER // LANE):
                at = slice(tile * LANE, (tile + 1) * LANE)
                basis_ref[index, pl.ds(first, step), at] = cosine.astype(bf16)
                basis_ref[index, pl.ds(PAIRS + first, step), at] = sine.astype(bf16)
                cosine, sine = cosine * turn_cos - sine * turn_sin, sine * turn_cos + cosine * turn_sin
            return carry

        lax.fori_loop(0, PAIRS // step, rows_of, 0)


def fourier_kernel(
    me_ref, lat_owner_ref, lat_points_ref, received_ref, scale_ref, basis_ref, out_ref, wide, narrow, left, quarters, grid
):
    points = my_points(me_ref, lat_owner_ref, lat_points_ref)
    quarter = points // 4
    for source in range(N_WAVE):
        for part in range(SLOTS // 4):
            wide[pl.ds(source * 24 + 4 * part, 4), :] = received_ref[source, part].astype(f32)
    for slot in range(SLOTS):
        narrow[slot * N_WAVE : (slot + 1) * N_WAVE, :] = wide[pl.ds(slot, N_WAVE, stride=24), :].astype(bf16)
    out_row, in_col = iota((COLS, COLS), 0), iota((COLS, COLS), 1)
    turn = jnp.where(in_col == 2 * (out_row % LEVELS) + out_row // LEVELS, 1.0, 0.0).astype(bf16)
    for index in range(2):
        turned = lax.dot_general(
            turn,
            narrow[index * PAIRS : (index + 1) * PAIRS, :],
            (((1,), (1,)), ((), ())),
            preferred_element_type=f32,
        )
        weighted = turned * scale_ref[2 * index : 2 * index + 1, :]
        signed = turned * scale_ref[2 * index + 1 : 2 * index + 2, :]
        left[index, :LEVELS, :PAIRS] = weighted[:LEVELS].astype(bf16)
        left[index, :LEVELS, PAIRS:] = weighted[LEVELS:].astype(bf16)
        if index == 0:
            left[index, LEVELS:, :PAIRS] = signed[:LEVELS].astype(bf16)
            left[index, LEVELS:, PAIRS:] = signed[LEVELS:].astype(bf16)
        else:
            left[index, LEVELS:, :PAIRS] = signed[LEVELS:].astype(bf16)
            left[index, LEVELS:, PAIRS:] = -signed[:LEVELS].astype(bf16)
    for first in range(0, QUARTER, 256):
        at = slice(first, min(first + 256, QUARTER))
        even = jnp.dot(left[0], basis_ref[0, :, at], preferred_element_type=f32)
        odd = jnp.dot(left[1], basis_ref[1, :, at], preferred_element_type=f32)
        valid = iota((1, even.shape[1]), 1) + first < quarter
        even = jnp.where(valid, even, 0.0)
        odd = jnp.where(valid, odd, 0.0)
        grid[:, at] = even[:LEVELS] + odd[:LEVELS]
        quarters[0, :, at] = even[LEVELS:] - odd[LEVELS:]
        quarters[1, :, at] = even[:LEVELS] - odd[:LEVELS]
        quarters[2, :, at] = even[LEVELS:] + odd[LEVELS:]
    grid[:, QUARTER:] = jnp.zeros((LEVELS, NLON_PAD - QUARTER), f32)
    lane = iota((LEVELS, LANE), 1)
    for index in range(3):
        offset = (index + 1) * quarter
        base = pl.multiple_of(offset // LANE * LANE, LANE)
        shift = offset - base
        before = jnp.zeros((LEVELS, LANE), f32)
        for tile in range(QUARTER // LANE + 1):
            if tile < QUARTER // LANE:
                now = pltpu.roll(quarters[index, :, tile * LANE : (tile + 1) * LANE], shift, 1)
            else:
                now = jnp.zeros((LEVELS, LANE), f32)
            at = pl.ds(base + tile * LANE, LANE)
            grid[:, at] = grid[:, at] + jnp.where(lane < shift, before, now)
            before = now
    out_ref[0] = grid[...].astype(bf16)


def params(mib):
    return pltpu.CompilerParams(vmem_limit_bytes=mib * 1024 * 1024)


def per_device(spectral, table, wave_owner, lat_owner, lat_points):
    me = lax.axis_index("wave").astype(jnp.int32).reshape(1)
    owner_row = wave_owner[:PAIRS].reshape(1, PAIRS)
    tables = lax.all_gather(table, "lev", axis=0, tiled=False)
    pairs, local = pl.pallas_call(
        slots_kernel,
        out_shape=(jax.ShapeDtypeStruct((8, PAIRS), f32), jax.ShapeDtypeStruct((16, LANE), f32)),
        in_specs=[SMEM, VMEM],
        out_specs=(VMEM, VMEM),
        name="slots",
    )(me, owner_row)
    four = pl.pallas_call(
        legendre_kernel,
        out_shape=jax.ShapeDtypeStruct((N_WAVE, SLOTS // 4, 4, COLS), bf16),
        in_specs=[SMEM, VMEM, VMEM, VMEM],
        out_specs=VMEM,
        scratch_shapes=[pltpu.VMEM((NORTH, ROWS_PAD), f32), pltpu.VMEM((SLOTS * NLAT, COLS), f32)],
        compiler_params=params(32),
        name="legendre",
    )(lat_owner, local, tables, spectral)
    received = lax.all_to_all(four, "wave", split_axis=0, concat_axis=0, tiled=True)
    basis, scale = pl.pallas_call(
        basis_kernel,
        out_shape=(
            jax.ShapeDtypeStruct((2, 2 * PAIRS, QUARTER), bf16),
            jax.ShapeDtypeStruct((8, PAIRS), f32),
        ),
        in_specs=[SMEM, SMEM, SMEM, VMEM, pl.BlockSpec(memory_space=pl.ANY)],
        out_specs=(VMEM, VMEM),
        scratch_shapes=[pltpu.VMEM((2 * PAIRS, LANE), f32)],
        compiler_params=params(24),
        name="basis",
    )(me, lat_owner, lat_points, pairs, four)
    return pl.pallas_call(
        fourier_kernel,
        out_shape=jax.ShapeDtypeStruct((1, LEVELS, NLON_PAD), bf16),
        in_specs=[SMEM, SMEM, SMEM, VMEM, VMEM, VMEM],
        out_specs=VMEM,
        scratch_shapes=[
            pltpu.VMEM((N_WAVE * 24, COLS), f32),
            pltpu.VMEM((SLOTS * N_WAVE, COLS), bf16),
            pltpu.VMEM((2, COLS, 2 * PAIRS), bf16),
            pltpu.VMEM((3, LEVELS, QUARTER), f32),
            pltpu.VMEM((LEVELS, NLON_PAD), f32),
        ],
        compiler_params=params(32),
        name="fourier",
    )(me, lat_owner, lat_points, received, scale, basis)


def solution(mesh):
    in_specs = (P("wave", "lev"), P("lev", "wave"), P(), P(), P())
    out_specs = P("wave", "lev", None)
    return jax.shard_map(
        per_device, mesh=mesh, in_specs=in_specs, out_specs=out_specs, check_vma=False
    )
```

```python
import math

import jax
import jax.numpy as jnp
from jax import lax
from jax.experimental import pallas as pl
from jax.experimental.pallas import tpu as pltpu
from jax.sharding import PartitionSpec as P

TRUNC = 1279
PAIRS = 640
PAIRS_DEV = 10
PAIR_ROWS = 1282
ROWS_DEV = 12820
ROWS_PAD = 12928
N_WAVE = 64
NLAT = 64
NORTH = 32
LEVELS = 64
COLS = 128
SLOTS = 20
QUARTER = 1408
NLON_PAD = 5376
LANE = 128

VMEM = pl.BlockSpec(memory_space=pltpu.VMEM)
SMEM = pl.BlockSpec(memory_space=pltpu.SMEM)
HBM = pl.BlockSpec(memory_space=pltpu.HBM)
f32 = jnp.float32
bf16 = jnp.bfloat16


def iota(shape, dim):
    return lax.broadcasted_iota(jnp.int32, shape, dim)


def to_column(row):
    eye = iota((LANE, LANE), 0) == iota((LANE, LANE), 1)
    parts = []
    for first in range(0, row.shape[1], LANE):
        block = jnp.broadcast_to(row[:, first : first + LANE], (LANE, LANE))
        parts.append(jnp.sum(jnp.where(eye, block, 0.0), axis=1, keepdims=True))
    return jnp.concatenate(parts, axis=0)


def slot_pairs(owner_row):
    owner_col = to_column(owner_row)
    pair_row = iota((1, PAIRS), 1)
    rank = jnp.zeros((1, PAIRS), f32)
    for first in range(0, PAIRS, LANE):
        same = owner_col[first : first + LANE] == owner_row
        earlier = (iota((LANE, PAIRS), 0) + first) < pair_row
        rank += jnp.sum(jnp.where(same & earlier, 1.0, 0.0), axis=0, keepdims=True)
    slot_col = to_column(rank * N_WAVE + owner_row)
    slot_row = iota((1, PAIRS), 1).astype(f32)
    pairs = jnp.zeros((1, PAIRS), f32)
    for first in range(0, PAIRS, LANE):
        here = slot_col[first : first + LANE] == slot_row
        pair = (iota((LANE, PAIRS), 0) + first).astype(f32)
        pairs += jnp.sum(jnp.where(here, pair, 0.0), axis=0, keepdims=True)
    return pairs


def is_odd(value):
    return value - 2.0 * jnp.floor(value * 0.5)


def owner_rows(owner_ref):
    return [owner_ref[pl.ds(first, LANE)].reshape(1, LANE).astype(f32) for first in range(0, PAIRS, LANE)]


def local_pairs(rows, me):
    count = len(rows)
    own = jnp.concatenate([jnp.where(row == me, 1.0, 0.0) for row in rows], axis=0)
    pair = (iota((count, LANE), 0) * LANE + iota((count, LANE), 1)).astype(f32)
    before = jnp.where(iota((LANE, LANE), 0) < iota((LANE, LANE), 1), 1.0, 0.0).astype(bf16)
    rank = jnp.dot(own.astype(bf16), before, preferred_element_type=f32)
    totals = jnp.sum(own, axis=1, keepdims=True)
    carry = jnp.zeros((1, 1), f32)
    carries = []
    for index in range(count):
        carries.append(carry)
        carry = carry + totals[index : index + 1]
    rank = jnp.where(own > 0, rank + jnp.concatenate(carries, axis=0), -1.0)
    return [
        jnp.sum(jnp.sum(jnp.where(rank == index, pair, 0.0), axis=1, keepdims=True), axis=0, keepdims=True)
        for index in range(PAIRS_DEV)
    ]


def first_row(pair):
    return PAIR_ROWS * pair // LANE * LANE


def last_row(pair):
    return min(-(-PAIR_ROWS * (pair + 1) // LANE) * LANE, ROWS_DEV)


def legendre_kernel(
    me_ref, owner_hbm, lat_owner_hbm, table_ref, spectral_hbm, out_ref, owner, lat_owner, table, spectral, four, small, large
):
    copies = [
        pltpu.make_async_copy(owner_hbm, owner, small.at[0]),
        pltpu.make_async_copy(lat_owner_hbm, lat_owner, small.at[1]),
    ]
    pieces = []
    for pair in range(PAIRS_DEV):
        start = last_row(pair - 1) if pair else 0
        at = pl.ds(start, last_row(pair) - start)
        pieces.append(pltpu.make_async_copy(spectral_hbm.at[at], spectral.at[at], large.at[pair]))
    for copy in copies + pieces:
        copy.start()
    for index in range(8):
        table[4 * index : 4 * index + 4, 0:ROWS_DEV] = table_ref[index].astype(f32)
    copies[0].wait()
    locals_ = local_pairs(owner_rows(owner), me_ref[0].astype(f32))
    for pair in range(PAIRS_DEV):
        start, stop = first_row(pair), last_row(pair)
        width = stop - start
        row = (iota((1, width), 1) + (start - PAIR_ROWS * pair)).astype(f32)
        q = locals_[pair]
        q_odd = is_odd(q)
        split = TRUNC + 1 - q
        low = jnp.where((row >= 0) & (row < split), 1.0, 0.0)
        high = jnp.where((row >= split) & (row < TRUNC + 2), 1.0, 0.0)
        even = jnp.where(q_odd > 0, high, low)
        odd = low + high - even
        odd_sign = 1.0 - 2.0 * is_odd(row)
        even_sign = odd_sign * (1.0 - 2.0 * q_odd)
        block = table[:, start:stop]
        left = jnp.concatenate(
            [block * even, block * (even * even_sign), block * odd, block * (odd * odd_sign)], axis=0
        ).astype(bf16)
        if pair in (0, 5):
            for piece in pieces[pair : pair + 5]:
                piece.wait()
        values = jnp.dot(left, spectral[start:stop, :], preferred_element_type=f32)
        four[pair * NLAT : (pair + 1) * NLAT, :] = values[:NLAT]
        four[(PAIRS_DEV + pair) * NLAT : (PAIRS_DEV + pair + 1) * NLAT, :] = values[NLAT:]
    copies[1].wait()
    for latitude in range(NLAT):
        to = lat_owner[latitude]
        for part in range(SLOTS // 4):
            rows = four[pl.ds(4 * part * NLAT + latitude, 4, stride=NLAT), :]
            out_ref[to, part] = rows.astype(bf16)


def circle(quarters_per_turn, numerator, inverse):
    turns = jnp.floor(numerator * inverse + 0.5)
    v = (numerator - turns * quarters_per_turn) * inverse
    z = v * v
    h = math.pi / 2
    sine = v * (h + z * (-(h**3) / 6 + z * (h**5 / 120 + z * (-(h**7) / 5040))))
    cosine = 1.0 + z * (-(h**2) / 2 + z * (h**4 / 24 + z * (-(h**6) / 720 + z * (h**8 / 40320))))
    halves = jnp.floor(turns * 0.5)
    odd_turn = turns - 2.0 * halves
    flip = 1.0 - 2.0 * is_odd(halves)
    swap = odd_turn > 0.5
    out_cos = jnp.where(swap, sine, cosine) * (flip * (1.0 - 2.0 * odd_turn))
    out_sin = jnp.where(swap, cosine, sine) * flip
    return out_cos, -out_sin


def my_points(me_ref, lat_owner, lat_points):
    latitude = jnp.int32(0)
    for index in range(NLAT):
        latitude = jnp.where(lat_owner[index] == me_ref[0], index % NORTH, latitude)
    return lat_points[latitude]


TILES = QUARTER // LANE
KEPT = 4
STEP = 32


def basis_kernel(
    me_ref, owner_hbm, lat_owner_hbm, lat_points_hbm, after_hbm, near, far_hbm, scale,
    owner, lat_owner, lat_points, waves, far, small, large,
):
    del after_hbm
    copies = [
        pltpu.make_async_copy(owner_hbm, owner, small.at[0]),
        pltpu.make_async_copy(lat_owner_hbm, lat_owner, small.at[1]),
        pltpu.make_async_copy(lat_points_hbm, lat_points, small.at[2]),
    ]
    for copy in copies:
        copy.start()
    for copy in copies:
        copy.wait()
    points = my_points(me_ref, lat_owner, lat_points)
    pair = slot_pairs(jnp.concatenate(owner_rows(owner), axis=1))
    even = jnp.where(is_odd(pair) > 0, TRUNC - pair, pair)
    for index, wave in enumerate((even, TRUNC - even)):
        weight = jnp.where(wave == 0, 1.0, 2.0) * jnp.where(2.0 * wave < points.astype(f32), 1.0, 0.0)
        sign = 1.0 - 2.0 * is_odd(jnp.floor(wave * 0.5))
        scale[2 * index : 2 * index + 1, :] = weight
        scale[2 * index + 1 : 2 * index + 2, :] = weight * sign
        waves[index * PAIRS : (index + 1) * PAIRS, :] = jnp.broadcast_to(to_column(wave), (PAIRS, LANE))
    scale[4:8, :] = jnp.zeros((4, PAIRS), f32)
    quarter = jnp.full((1, LANE), (points // 4).astype(f32))
    inverse = 1.0 / quarter
    column = iota((STEP, LANE), 1).astype(f32)
    outs = []
    for index in range(2):

        def rows_of(block, carry):
            first = pl.multiple_of(block * STEP, STEP)
            wave = waves[pl.ds(index * PAIRS + first, STEP), :]
            cosine, sine = circle(quarter, wave * column, inverse)
            turn_cos, turn_sin = circle(quarter, wave * float(LANE), inverse)
            for tile in range(TILES):
                basis, at = (near, tile) if tile < KEPT else (far, tile - KEPT)
                basis[at, index, pl.ds(first, STEP), :] = cosine.astype(bf16)
                basis[at, index, pl.ds(PAIRS + first, STEP), :] = sine.astype(bf16)
                cosine, sine = cosine * turn_cos - sine * turn_sin, sine * turn_cos + cosine * turn_sin
            return carry

        lax.fori_loop(0, PAIRS // STEP, rows_of, 0)
        for tile in range(TILES - KEPT):
            at = large.at[index * (TILES - KEPT) + tile]
            outs.append(pltpu.make_async_copy(far.at[tile, index], far_hbm.at[tile, index], at))
            outs[-1].start()
    for copy in outs:
        copy.wait()


def fourier_kernel(
    me_ref, lat_owner_hbm, lat_points_hbm, received_ref, scale, near, far_hbm, out_ref,
    lat_owner, lat_points, far, wide, narrow, left, quarters, grid, small, large,
):
    copies = [
        pltpu.make_async_copy(lat_owner_hbm, lat_owner, small.at[0]),
        pltpu.make_async_copy(lat_points_hbm, lat_points, small.at[1]),
    ]
    pieces = [pltpu.make_async_copy(far_hbm.at[tile], far.at[tile], large.at[tile]) for tile in range(TILES - KEPT)]
    for copy in copies + pieces:
        copy.start()
    grid[:, QUARTER:] = jnp.zeros((LEVELS, NLON_PAD - QUARTER), f32)
    for source in range(N_WAVE):
        for part in range(SLOTS // 4):
            wide[pl.ds(source * 24 + 4 * part, 4), :] = received_ref[source, part].astype(f32)
    for slot in range(SLOTS):
        narrow[slot * N_WAVE : (slot + 1) * N_WAVE, :] = wide[pl.ds(slot, N_WAVE, stride=24), :].astype(bf16)
    for copy in copies:
        copy.wait()
    quarter = my_points(me_ref, lat_owner, lat_points) // 4
    out_row, in_col = iota((COLS, COLS), 0), iota((COLS, COLS), 1)
    turn = jnp.where(in_col == 2 * (out_row % LEVELS) + out_row // LEVELS, 1.0, 0.0).astype(bf16)
    for index in range(2):
        turned = lax.dot_general(
            turn,
            narrow[index * PAIRS : (index + 1) * PAIRS, :],
            (((1,), (1,)), ((), ())),
            preferred_element_type=f32,
        )
        weighted = turned * scale[2 * index : 2 * index + 1, :]
        signed = turned * scale[2 * index + 1 : 2 * index + 2, :]
        left[index, :LEVELS, :PAIRS] = weighted[:LEVELS].astype(bf16)
        left[index, :LEVELS, PAIRS:] = weighted[LEVELS:].astype(bf16)
        if index == 0:
            left[index, LEVELS:, :PAIRS] = signed[:LEVELS].astype(bf16)
            left[index, LEVELS:, PAIRS:] = signed[LEVELS:].astype(bf16)
        else:
            left[index, LEVELS:, :PAIRS] = signed[LEVELS:].astype(bf16)
            left[index, LEVELS:, PAIRS:] = -signed[:LEVELS].astype(bf16)
    for first in range(0, QUARTER, 256):
        at = slice(first, min(first + 256, QUARTER))
        tiles = range(first // LANE, at.stop // LANE)
        if tiles.start == KEPT:
            for piece in pieces:
                piece.wait()
        even, odd = [
            jnp.dot(
                left[index],
                jnp.concatenate(
                    [near[tile, index] if tile < KEPT else far[tile - KEPT, index] for tile in tiles], axis=1
                ),
                preferred_element_type=f32,
            )
            for index in range(2)
        ]
        valid = iota((1, even.shape[1]), 1) + first < quarter
        even = jnp.where(valid, even, 0.0)
        odd = jnp.where(valid, odd, 0.0)
        grid[:, at] = even[:LEVELS] + odd[:LEVELS]
        quarters[0, :, at] = even[LEVELS:] - odd[LEVELS:]
        quarters[1, :, at] = even[:LEVELS] - odd[:LEVELS]
        quarters[2, :, at] = even[LEVELS:] + odd[LEVELS:]
    lane = iota((LEVELS, LANE), 1)
    for index in range(3):
        offset = (index + 1) * quarter
        base = pl.multiple_of(offset // LANE * LANE, LANE)
        shift = offset - base
        before = jnp.zeros((LEVELS, LANE), f32)
        for tile in range(QUARTER // LANE + 1):
            if tile < QUARTER // LANE:
                now = pltpu.roll(quarters[index, :, tile * LANE : (tile + 1) * LANE], shift, 1)
            else:
                now = jnp.zeros((LEVELS, LANE), f32)
            at = pl.ds(base + tile * LANE, LANE)
            grid[:, at] = grid[:, at] + jnp.where(lane < shift, before, now)
            before = now
    out_ref[0] = grid[...].astype(bf16)


def params(mib):
    return pltpu.CompilerParams(vmem_limit_bytes=mib * 1024 * 1024)


def per_device(spectral, table, wave_owner, lat_owner, lat_points):
    me = lax.axis_index("wave").astype(jnp.int32).reshape(1)
    waves = wave_owner.shape[0]
    tables = lax.all_gather(table, "lev", axis=0, tiled=False)
    spectral, wave_owner, lat_owner, lat_points = [
        pltpu.with_memory_space_constraint(array, pltpu.HBM)
        for array in (spectral, wave_owner, lat_owner, lat_points)
    ]
    owner_scratch = pltpu.VMEM((waves,), jnp.int32)
    lat_owner_scratch = pltpu.SMEM((NLAT,), jnp.int32)
    lat_points_scratch = pltpu.SMEM((NORTH,), jnp.int32)
    dma = pltpu.SemaphoreType.DMA
    four = pl.pallas_call(
        legendre_kernel,
        out_shape=jax.ShapeDtypeStruct((N_WAVE, SLOTS // 4, 4, COLS), bf16),
        in_specs=[SMEM, HBM, HBM, VMEM, HBM],
        out_specs=VMEM,
        scratch_shapes=[
            owner_scratch,
            lat_owner_scratch,
            pltpu.VMEM((NORTH, ROWS_PAD), f32),
            pltpu.VMEM((ROWS_DEV, COLS), bf16),
            pltpu.VMEM((SLOTS * NLAT, COLS), f32),
            dma((2,)),
            dma((PAIRS_DEV,)),
        ],
        compiler_params=params(24),
        name="legendre",
    )(me, wave_owner, lat_owner, tables, spectral)
    received = lax.all_to_all(four, "wave", split_axis=0, concat_axis=0, tiled=True)
    near_shape = (KEPT, 2, 2 * PAIRS, LANE)
    far_shape = (TILES - KEPT, 2, 2 * PAIRS, LANE)
    near, far, scale = pl.pallas_call(
        basis_kernel,
        out_shape=(pltpu.VMEM(near_shape, bf16), pltpu.HBM(far_shape, bf16), pltpu.VMEM((8, PAIRS), f32)),
        in_specs=[SMEM, HBM, HBM, HBM, HBM],
        out_specs=(VMEM, HBM, VMEM),
        scratch_shapes=[
            owner_scratch,
            lat_owner_scratch,
            lat_points_scratch,
            pltpu.VMEM((2 * PAIRS, LANE), f32),
            pltpu.VMEM(far_shape, bf16),
            dma((3,)),
            dma((2 * (TILES - KEPT),)),
        ],
        compiler_params=params(16),
        name="basis",
    )(me, wave_owner, lat_owner, lat_points, pltpu.with_memory_space_constraint(four, pltpu.HBM))
    return pl.pallas_call(
        fourier_kernel,
        out_shape=jax.ShapeDtypeStruct((1, LEVELS, NLON_PAD), bf16),
        in_specs=[SMEM, HBM, HBM, VMEM, VMEM, VMEM, HBM],
        out_specs=VMEM,
        scratch_shapes=[
            lat_owner_scratch,
            lat_points_scratch,
            pltpu.VMEM(far_shape, bf16),
            pltpu.VMEM((N_WAVE * 24, COLS), f32),
            pltpu.VMEM((SLOTS * N_WAVE, COLS), bf16),
            pltpu.VMEM((2, COLS, 2 * PAIRS), bf16),
            pltpu.VMEM((3, LEVELS, QUARTER), f32),
            pltpu.VMEM((LEVELS, NLON_PAD), f32),
            dma((2,)),
            dma((TILES - KEPT,)),
        ],
        compiler_params=params(24),
        name="fourier",
    )(
        me,
        lat_owner,
        lat_points,
        received,
        pltpu.with_memory_space_constraint(scale, pltpu.VMEM),
        pltpu.with_memory_space_constraint(near, pltpu.VMEM),
        pltpu.with_memory_space_constraint(far, pltpu.HBM),
    )


def solution(mesh):
    in_specs = (P("wave", "lev"), P("lev", "wave"), P(), P(), P())
    out_specs = P("wave", "lev", None)
    return jax.shard_map(
        per_device, mesh=mesh, in_specs=in_specs, out_specs=out_specs, check_vma=False
    )
```

```python
import math

import jax
import jax.numpy as jnp
from jax import lax
from jax.experimental import pallas as pl
from jax.experimental.pallas import tpu as pltpu
from jax.sharding import PartitionSpec as P

TRUNC = 1279
PAIRS = 640
PAIRS_DEV = 10
PAIR_ROWS = 1282
ROWS_DEV = 12820
ROWS_PAD = 12928
N_WAVE = 64
NLAT = 64
NORTH = 32
LEVELS = 64
COLS = 128
SLOTS = 20
EIGHTH = 768
NLON_PAD = 5376
LANE = 128

VMEM = pl.BlockSpec(memory_space=pltpu.VMEM)
SMEM = pl.BlockSpec(memory_space=pltpu.SMEM)
HBM = pl.BlockSpec(memory_space=pltpu.HBM)
f32 = jnp.float32
bf16 = jnp.bfloat16


def iota(shape, dim):
    return lax.broadcasted_iota(jnp.int32, shape, dim)


def to_column(row):
    eye = iota((LANE, LANE), 0) == iota((LANE, LANE), 1)
    parts = []
    for first in range(0, row.shape[1], LANE):
        block = jnp.broadcast_to(row[:, first : first + LANE], (LANE, LANE))
        parts.append(jnp.sum(jnp.where(eye, block, 0.0), axis=1, keepdims=True))
    return jnp.concatenate(parts, axis=0)


def slot_pairs(owner_row):
    owner_col = to_column(owner_row)
    pair_row = iota((1, PAIRS), 1)
    rank = jnp.zeros((1, PAIRS), f32)
    for first in range(0, PAIRS, LANE):
        same = owner_col[first : first + LANE] == owner_row
        earlier = (iota((LANE, PAIRS), 0) + first) < pair_row
        rank += jnp.sum(jnp.where(same & earlier, 1.0, 0.0), axis=0, keepdims=True)
    slot_col = to_column(rank * N_WAVE + owner_row)
    slot_row = iota((1, PAIRS), 1).astype(f32)
    pairs = jnp.zeros((1, PAIRS), f32)
    for first in range(0, PAIRS, LANE):
        here = slot_col[first : first + LANE] == slot_row
        pair = (iota((LANE, PAIRS), 0) + first).astype(f32)
        pairs += jnp.sum(jnp.where(here, pair, 0.0), axis=0, keepdims=True)
    return pairs


def is_odd(value):
    return value - 2.0 * jnp.floor(value * 0.5)


def owner_rows(owner_ref):
    return [owner_ref[pl.ds(first, LANE)].reshape(1, LANE).astype(f32) for first in range(0, PAIRS, LANE)]


def local_pairs(rows, me):
    count = len(rows)
    own = jnp.concatenate([jnp.where(row == me, 1.0, 0.0) for row in rows], axis=0)
    pair = (iota((count, LANE), 0) * LANE + iota((count, LANE), 1)).astype(f32)
    before = jnp.where(iota((LANE, LANE), 0) < iota((LANE, LANE), 1), 1.0, 0.0).astype(bf16)
    rank = jnp.dot(own.astype(bf16), before, preferred_element_type=f32)
    totals = jnp.sum(own, axis=1, keepdims=True)
    carry = jnp.zeros((1, 1), f32)
    carries = []
    for index in range(count):
        carries.append(carry)
        carry = carry + totals[index : index + 1]
    rank = jnp.where(own > 0, rank + jnp.concatenate(carries, axis=0), -1.0)
    return [
        jnp.sum(jnp.sum(jnp.where(rank == index, pair, 0.0), axis=1, keepdims=True), axis=0, keepdims=True)
        for index in range(PAIRS_DEV)
    ]


def first_row(pair):
    return PAIR_ROWS * pair // LANE * LANE


def last_row(pair):
    return min(-(-PAIR_ROWS * (pair + 1) // LANE) * LANE, ROWS_DEV)


def legendre_kernel(
    me_ref, owner_hbm, lat_owner_hbm, table_ref, spectral_hbm, out_ref, owner, lat_owner, table, spectral, four, small, large
):
    copies = [
        pltpu.make_async_copy(owner_hbm, owner, small.at[0]),
        pltpu.make_async_copy(lat_owner_hbm, lat_owner, small.at[1]),
    ]
    pieces = []
    for pair in range(PAIRS_DEV):
        start = last_row(pair - 1) if pair else 0
        at = pl.ds(start, last_row(pair) - start)
        pieces.append(pltpu.make_async_copy(spectral_hbm.at[at], spectral.at[at], large.at[pair]))
    for copy in copies + pieces:
        copy.start()
    for index in range(8):
        table[4 * index : 4 * index + 4, 0:ROWS_DEV] = table_ref[index].astype(f32)
    copies[0].wait()
    locals_ = local_pairs(owner_rows(owner), me_ref[0].astype(f32))
    for pair in range(PAIRS_DEV):
        start, stop = first_row(pair), last_row(pair)
        width = stop - start
        row = (iota((1, width), 1) + (start - PAIR_ROWS * pair)).astype(f32)
        q = locals_[pair]
        q_odd = is_odd(q)
        split = TRUNC + 1 - q
        low = jnp.where((row >= 0) & (row < split), 1.0, 0.0)
        high = jnp.where((row >= split) & (row < TRUNC + 2), 1.0, 0.0)
        even = jnp.where(q_odd > 0, high, low)
        odd = low + high - even
        odd_sign = 1.0 - 2.0 * is_odd(row)
        even_sign = odd_sign * (1.0 - 2.0 * q_odd)
        block = table[:, start:stop]
        left = jnp.concatenate(
            [block * even, block * (even * even_sign), block * odd, block * (odd * odd_sign)], axis=0
        ).astype(bf16)
        if pair in (0, 5):
            for piece in pieces[pair : pair + 5]:
                piece.wait()
        values = jnp.dot(left, spectral[start:stop, :], preferred_element_type=f32)
        four[pair * NLAT : (pair + 1) * NLAT, :] = values[:NLAT]
        four[(PAIRS_DEV + pair) * NLAT : (PAIRS_DEV + pair + 1) * NLAT, :] = values[NLAT:]
    copies[1].wait()
    for latitude in range(NLAT):
        to = lat_owner[latitude]
        for part in range(SLOTS // 4):
            rows = four[pl.ds(4 * part * NLAT + latitude, 4, stride=NLAT), :]
            out_ref[to, part] = rows.astype(bf16)


def circle(quarters_per_turn, numerator, inverse):
    turns = jnp.floor(numerator * inverse + 0.5)
    v = (numerator - turns * quarters_per_turn) * inverse
    z = v * v
    h = math.pi / 2
    sine = v * (h + z * (-(h**3) / 6 + z * (h**5 / 120 + z * (-(h**7) / 5040))))
    cosine = 1.0 + z * (-(h**2) / 2 + z * (h**4 / 24 + z * (-(h**6) / 720 + z * (h**8 / 40320))))
    halves = jnp.floor(turns * 0.5)
    odd_turn = turns - 2.0 * halves
    flip = 1.0 - 2.0 * is_odd(halves)
    swap = odd_turn > 0.5
    out_cos = jnp.where(swap, sine, cosine) * (flip * (1.0 - 2.0 * odd_turn))
    out_sin = jnp.where(swap, cosine, sine) * flip
    return out_cos, -out_sin


def my_points(me_ref, lat_owner, lat_points):
    latitude = jnp.int32(0)
    for index in range(NLAT):
        latitude = jnp.where(lat_owner[index] == me_ref[0], index % NORTH, latitude)
    return lat_points[latitude]


TILES = EIGHTH // LANE
MARGIN = TILES + 1
GROUP = 32
KEPT = 4
STEP = 32


def basis_kernel(
    me_ref, owner_hbm, lat_owner_hbm, lat_points_hbm, after_hbm, near, far_hbm, scale,
    owner, lat_owner, lat_points, waves, far, small, large,
):
    del after_hbm
    copies = [
        pltpu.make_async_copy(owner_hbm, owner, small.at[0]),
        pltpu.make_async_copy(lat_owner_hbm, lat_owner, small.at[1]),
        pltpu.make_async_copy(lat_points_hbm, lat_points, small.at[2]),
    ]
    for copy in copies:
        copy.start()
    for copy in copies:
        copy.wait()
    points = my_points(me_ref, lat_owner, lat_points)
    pair = slot_pairs(jnp.concatenate(owner_rows(owner), axis=1))
    even = jnp.where(is_odd(pair) > 0, TRUNC - pair, pair)
    for index, wave in enumerate((even, TRUNC - even)):
        weight = jnp.where(wave == 0, 1.0, 2.0) * jnp.where(2.0 * wave < points.astype(f32), 1.0, 0.0)
        sign = 1.0 - 2.0 * is_odd(jnp.floor(wave * 0.5))
        scale[2 * index : 2 * index + 1, :] = weight
        scale[2 * index + 1 : 2 * index + 2, :] = weight * sign
        waves[index * PAIRS : (index + 1) * PAIRS, :] = jnp.broadcast_to(to_column(wave), (PAIRS, LANE))
    scale[4:8, :] = jnp.zeros((4, PAIRS), f32)
    quarter = jnp.full((1, LANE), (points // 4).astype(f32))
    inverse = 1.0 / quarter
    column = iota((STEP, LANE), 1).astype(f32)
    outs = []
    for index in range(2):

        def rows_of(block, carry):
            first = pl.multiple_of(block * STEP, STEP)
            wave = waves[pl.ds(index * PAIRS + first, STEP), :]
            cosine, sine = circle(quarter, wave * column, inverse)
            turn_cos, turn_sin = circle(quarter, wave * float(LANE), inverse)
            for tile in range(TILES):
                basis, at = (near, tile) if tile < KEPT else (far, tile - KEPT)
                basis[at, index, pl.ds(first, STEP), :] = cosine.astype(bf16)
                basis[at, index, pl.ds(PAIRS + first, STEP), :] = sine.astype(bf16)
                cosine, sine = cosine * turn_cos - sine * turn_sin, sine * turn_cos + cosine * turn_sin
            return carry

        lax.fori_loop(0, PAIRS // STEP, rows_of, 0)
        for tile in range(TILES - KEPT):
            at = large.at[index * (TILES - KEPT) + tile]
            outs.append(pltpu.make_async_copy(far.at[tile, index], far_hbm.at[tile, index], at))
            outs[-1].start()
    for copy in outs:
        copy.wait()


def fourier_kernel(
    me_ref, lat_owner_hbm, lat_points_hbm, received_ref, scale, near, far_hbm, out_hbm,
    lat_owner, lat_points, far, wide, narrow, left, ahead, back, grid, rounded, small, large,
):
    copies = [
        pltpu.make_async_copy(lat_owner_hbm, lat_owner, small.at[0]),
        pltpu.make_async_copy(lat_points_hbm, lat_points, small.at[1]),
    ]
    pieces = [pltpu.make_async_copy(far_hbm.at[tile], far.at[tile], large.at[tile]) for tile in range(TILES - KEPT)]
    for copy in copies + pieces:
        copy.start()
    grid[...] = jnp.zeros(grid.shape, f32)
    for source in range(N_WAVE):
        for part in range(SLOTS // 4):
            wide[pl.ds(source * 24 + 4 * part, 4), :] = received_ref[source, part].astype(f32)
    for slot in range(SLOTS):
        narrow[slot * N_WAVE : (slot + 1) * N_WAVE, :] = wide[pl.ds(slot, N_WAVE, stride=24), :].astype(bf16)
    out_row, in_col = iota((COLS, COLS), 0), iota((COLS, COLS), 1)
    turn = jnp.where(in_col == 2 * (out_row % LEVELS) + out_row // LEVELS, 1.0, 0.0).astype(bf16)
    for index in range(2):
        turned = lax.dot_general(
            turn,
            narrow[index * PAIRS : (index + 1) * PAIRS, :],
            (((1,), (1,)), ((), ())),
            preferred_element_type=f32,
        )
        weighted = turned * scale[2 * index : 2 * index + 1, :]
        signed = turned * scale[2 * index + 1 : 2 * index + 2, :]
        left[index, 0, :LEVELS] = weighted[:LEVELS].astype(bf16)
        left[index, 1, :LEVELS] = weighted[LEVELS:].astype(bf16)
        if index == 0:
            left[index, 0, LEVELS:] = signed[:LEVELS].astype(bf16)
            left[index, 1, LEVELS:] = signed[LEVELS:].astype(bf16)
        else:
            left[index, 0, LEVELS:] = signed[LEVELS:].astype(bf16)
            left[index, 1, LEVELS:] = -signed[:LEVELS].astype(bf16)
    for copy in copies:
        copy.wait()
    quarter = my_points(me_ref, lat_owner, lat_points) // 4
    half = quarter // 2
    for first in range(0, EIGHTH, 2 * LANE):
        at = slice(first, first + 2 * LANE)
        tiles = range(first // LANE, first // LANE + 2)
        if tiles.start == KEPT:
            for piece in pieces:
                piece.wait()
        sums = []
        for index in range(2):
            right = jnp.concatenate(
                [near[tile, index] if tile < KEPT else far[tile - KEPT, index] for tile in tiles], axis=1
            )
            sums.append(jnp.dot(left[index, 0], right[:PAIRS], preferred_element_type=f32))
            sums.append(jnp.dot(left[index, 1], right[PAIRS:], preferred_element_type=f32))
        even_cos, even_sin, odd_cos, odd_sin = sums
        even, odd = even_cos + even_sin, odd_cos + odd_sin
        ahead[0, :, at] = even[:LEVELS] + odd[:LEVELS]
        ahead[1, :, at] = even[LEVELS:] - odd[LEVELS:]
        ahead[2, :, at] = even[:LEVELS] - odd[:LEVELS]
        ahead[3, :, at] = even[LEVELS:] + odd[LEVELS:]
        even, odd = even_cos - even_sin, odd_cos - odd_sin
        back[0, :, at] = even[LEVELS:] - odd[LEVELS:]
        back[1, :, at] = even[:LEVELS] - odd[:LEVELS]
        back[2, :, at] = even[LEVELS:] + odd[LEVELS:]
        back[3, :, at] = even[:LEVELS] + odd[:LEVELS]
    lane = iota((GROUP, LANE), 1)
    zero = jnp.zeros((GROUP, LANE), f32)
    outs = []
    for group in range(LEVELS // GROUP):
        rows = slice(group * GROUP, (group + 1) * GROUP)

        def put(tile, value, first, last):
            at = pl.ds(pl.multiple_of((tile + MARGIN) * LANE, LANE), LANE)
            point = lane + tile * LANE
            pltpu.store(grid.at[rows, at], value, mask=(point >= first) & (point <= last))

        for index in range(4):
            offset = index * quarter
            shift = offset % LANE
            before = zero
            for tile in range(TILES + (1 if index else 0)):
                now = zero
                if tile < TILES:
                    now = ahead[index, rows, tile * LANE : (tile + 1) * LANE]
                    if index:
                        now = pltpu.roll(now, shift, 1)
                value = jnp.where(lane < shift, before, now) if index else now
                put(offset // LANE + tile, value, offset, offset + half)
                before = now
            offset = (index + 1) * quarter
            shift = offset % LANE
            order = lax.rem(shift - lane + LANE, LANE)
            before = zero
            for tile in range(TILES + 1):
                now = zero
                if tile < TILES:
                    now = jnp.take_along_axis(
                        back[index, rows, tile * LANE : (tile + 1) * LANE], order, axis=1, mode="promise_in_bounds"
                    )
                value = jnp.where(lane <= shift, now, before)
                put(offset // LANE - tile, value, index * quarter + half + 1, offset - 1)
                before = now
        rounded[rows, :] = grid[rows, MARGIN * LANE :].astype(bf16)
        at = pl.ds(group * GROUP, GROUP)
        outs.append(pltpu.make_async_copy(rounded.at[at], out_hbm.at[0, at], small.at[2 + group]))
        outs[-1].start()
    for copy in outs:
        copy.wait()


def params(mib):
    return pltpu.CompilerParams(vmem_limit_bytes=mib * 1024 * 1024)


def per_device(spectral, table, wave_owner, lat_owner, lat_points):
    me = lax.axis_index("wave").astype(jnp.int32).reshape(1)
    waves = wave_owner.shape[0]
    tables = lax.all_gather(table, "lev", axis=0, tiled=False)
    spectral, wave_owner, lat_owner, lat_points = [
        pltpu.with_memory_space_constraint(array, pltpu.HBM)
        for array in (spectral, wave_owner, lat_owner, lat_points)
    ]
    owner_scratch = pltpu.VMEM((waves,), jnp.int32)
    lat_owner_scratch = pltpu.SMEM((NLAT,), jnp.int32)
    lat_points_scratch = pltpu.SMEM((NORTH,), jnp.int32)
    dma = pltpu.SemaphoreType.DMA
    four = pl.pallas_call(
        legendre_kernel,
        out_shape=jax.ShapeDtypeStruct((N_WAVE, SLOTS // 4, 4, COLS), bf16),
        in_specs=[SMEM, HBM, HBM, VMEM, HBM],
        out_specs=VMEM,
        scratch_shapes=[
            owner_scratch,
            lat_owner_scratch,
            pltpu.VMEM((NORTH, ROWS_PAD), f32),
            pltpu.VMEM((ROWS_DEV, COLS), bf16),
            pltpu.VMEM((SLOTS * NLAT, COLS), f32),
            dma((2,)),
            dma((PAIRS_DEV,)),
        ],
        compiler_params=params(24),
        name="legendre",
    )(me, wave_owner, lat_owner, tables, spectral)
    received = lax.all_to_all(four, "wave", split_axis=0, concat_axis=0, tiled=True)
    near_shape = (KEPT, 2, 2 * PAIRS, LANE)
    far_shape = (TILES - KEPT, 2, 2 * PAIRS, LANE)
    near, far, scale = pl.pallas_call(
        basis_kernel,
        out_shape=(pltpu.VMEM(near_shape, bf16), pltpu.HBM(far_shape, bf16), pltpu.VMEM((8, PAIRS), f32)),
        in_specs=[SMEM, HBM, HBM, HBM, HBM],
        out_specs=(VMEM, HBM, VMEM),
        scratch_shapes=[
            owner_scratch,
            lat_owner_scratch,
            lat_points_scratch,
            pltpu.VMEM((2 * PAIRS, LANE), f32),
            pltpu.VMEM(far_shape, bf16),
            dma((3,)),
            dma((2 * (TILES - KEPT),)),
        ],
        compiler_params=params(16),
        name="basis",
    )(me, wave_owner, lat_owner, lat_points, pltpu.with_memory_space_constraint(four, pltpu.HBM))
    return pl.pallas_call(
        fourier_kernel,
        out_shape=pltpu.HBM((1, LEVELS, NLON_PAD), bf16),
        in_specs=[SMEM, HBM, HBM, VMEM, VMEM, VMEM, HBM],
        out_specs=HBM,
        scratch_shapes=[
            lat_owner_scratch,
            lat_points_scratch,
            pltpu.VMEM(far_shape, bf16),
            pltpu.VMEM((N_WAVE * 24, COLS), f32),
            pltpu.VMEM((SLOTS * N_WAVE, COLS), bf16),
            pltpu.VMEM((2, 2, COLS, PAIRS), bf16),
            pltpu.VMEM((4, LEVELS, EIGHTH), f32),
            pltpu.VMEM((4, LEVELS, EIGHTH), f32),
            pltpu.VMEM((LEVELS, MARGIN * LANE + NLON_PAD), f32),
            pltpu.VMEM((LEVELS, NLON_PAD), bf16),
            dma((2 + LEVELS // GROUP,)),
            dma((TILES - KEPT,)),
        ],
        compiler_params=params(24),
        name="fourier",
    )(
        me,
        lat_owner,
        lat_points,
        received,
        pltpu.with_memory_space_constraint(scale, pltpu.VMEM),
        pltpu.with_memory_space_constraint(near, pltpu.VMEM),
        pltpu.with_memory_space_constraint(far, pltpu.HBM),
    )


def solution(mesh):
    in_specs = (P("wave", "lev"), P("lev", "wave"), P(), P(), P())
    out_specs = P("wave", "lev", None)
    return jax.shard_map(
        per_device, mesh=mesh, in_specs=in_specs, out_specs=out_specs, check_vma=False
    )
```

```python
import math

import jax
import jax.numpy as jnp
from jax import lax
from jax.experimental import pallas as pl
from jax.experimental.pallas import tpu as pltpu
from jax.sharding import PartitionSpec as P

TRUNC = 1279
PAIRS = 640
PAIRS_DEV = 10
PAIR_ROWS = 1282
ROWS_DEV = 12820
ROWS_PAD = 12928
N_WAVE = 64
NLAT = 64
NORTH = 32
LEVELS = 64
COLS = 128
SLOTS = 20
EIGHTH = 768
NLON_PAD = 5376
LANE = 128

VMEM = pl.BlockSpec(memory_space=pltpu.VMEM)
SMEM = pl.BlockSpec(memory_space=pltpu.SMEM)
HBM = pl.BlockSpec(memory_space=pltpu.HBM)
f32 = jnp.float32
bf16 = jnp.bfloat16


def iota(shape, dim):
    return lax.broadcasted_iota(jnp.int32, shape, dim)


def to_column(row):
    eye = iota((LANE, LANE), 0) == iota((LANE, LANE), 1)
    parts = []
    for first in range(0, row.shape[1], LANE):
        block = jnp.broadcast_to(row[:, first : first + LANE], (LANE, LANE))
        parts.append(jnp.sum(jnp.where(eye, block, 0.0), axis=1, keepdims=True))
    return jnp.concatenate(parts, axis=0)


def slot_pairs(owner_row):
    owner_col = to_column(owner_row)
    pair_row = iota((1, PAIRS), 1)
    rank = jnp.zeros((1, PAIRS), f32)
    for first in range(0, PAIRS, LANE):
        same = owner_col[first : first + LANE] == owner_row
        earlier = (iota((LANE, PAIRS), 0) + first) < pair_row
        rank += jnp.sum(jnp.where(same & earlier, 1.0, 0.0), axis=0, keepdims=True)
    slot_col = to_column(rank * N_WAVE + owner_row)
    slot_row = iota((1, PAIRS), 1).astype(f32)
    pairs = jnp.zeros((1, PAIRS), f32)
    for first in range(0, PAIRS, LANE):
        here = slot_col[first : first + LANE] == slot_row
        pair = (iota((LANE, PAIRS), 0) + first).astype(f32)
        pairs += jnp.sum(jnp.where(here, pair, 0.0), axis=0, keepdims=True)
    return pairs


def is_odd(value):
    return value - 2.0 * jnp.floor(value * 0.5)


def owner_rows(owner_ref):
    return [owner_ref[pl.ds(first, LANE)].reshape(1, LANE).astype(f32) for first in range(0, PAIRS, LANE)]


def local_pairs(rows, me):
    count = len(rows)
    own = jnp.concatenate([jnp.where(row == me, 1.0, 0.0) for row in rows], axis=0)
    pair = (iota((count, LANE), 0) * LANE + iota((count, LANE), 1)).astype(f32)
    before = jnp.where(iota((LANE, LANE), 0) < iota((LANE, LANE), 1), 1.0, 0.0).astype(bf16)
    rank = jnp.dot(own.astype(bf16), before, preferred_element_type=f32)
    totals = jnp.sum(own, axis=1, keepdims=True)
    carry = jnp.zeros((1, 1), f32)
    carries = []
    for index in range(count):
        carries.append(carry)
        carry = carry + totals[index : index + 1]
    rank = jnp.where(own > 0, rank + jnp.concatenate(carries, axis=0), -1.0)
    return [
        jnp.sum(jnp.sum(jnp.where(rank == index, pair, 0.0), axis=1, keepdims=True), axis=0, keepdims=True)
        for index in range(PAIRS_DEV)
    ]


def first_row(pair):
    return PAIR_ROWS * pair // LANE * LANE


def last_row(pair):
    return min(-(-PAIR_ROWS * (pair + 1) // LANE) * LANE, ROWS_DEV)


PIECES = (0, 2, 5)


def legendre_kernel(
    me_ref, owner_hbm, lat_owner_hbm, table_ref, spectral_hbm, out_ref, owner, lat_owner, table, spectral, four, small, large
):
    copies = [
        pltpu.make_async_copy(owner_hbm, owner, small.at[0]),
        pltpu.make_async_copy(lat_owner_hbm, lat_owner, small.at[1]),
    ]
    pieces = {}
    for index, (pair, end) in enumerate(zip(PIECES, PIECES[1:] + (PAIRS_DEV,))):
        start = last_row(pair - 1) if pair else 0
        at = pl.ds(start, last_row(end - 1) - start)
        pieces[pair] = pltpu.make_async_copy(spectral_hbm.at[at], spectral.at[at], large.at[index])
    for copy in copies + list(pieces.values()):
        copy.start()
    for index in range(8):
        table[4 * index : 4 * index + 4, 0:ROWS_DEV] = table_ref[index].astype(f32)
    for copy in copies:
        copy.wait()
    locals_ = local_pairs(owner_rows(owner), me_ref[0].astype(f32))
    for pair in range(PAIRS_DEV):
        start, stop = first_row(pair), last_row(pair)
        width = stop - start
        row = (iota((1, width), 1) + (start - PAIR_ROWS * pair)).astype(f32)
        q = locals_[pair]
        q_odd = is_odd(q)
        split = TRUNC + 1 - q
        low = jnp.where((row >= 0) & (row < split), 1.0, 0.0)
        high = jnp.where((row >= split) & (row < TRUNC + 2), 1.0, 0.0)
        even = jnp.where(q_odd > 0, high, low)
        odd = low + high - even
        odd_sign = 1.0 - 2.0 * is_odd(row)
        even_sign = odd_sign * (1.0 - 2.0 * q_odd)
        block = table[:, start:stop].astype(bf16)
        left = jnp.concatenate(
            [block * mask.astype(bf16) for mask in (even, even * even_sign, odd, odd * odd_sign)], axis=0
        )
        if pair in pieces:
            pieces[pair].wait()
        values = jnp.dot(left, spectral[start:stop, :], preferred_element_type=f32)
        four[2 * pair * NLAT : 2 * (pair + 1) * NLAT, :] = values
        if pair % 2 == 1:
            part = pair // 2
            for latitude in range(NLAT):
                rows = four[pl.ds(4 * part * NLAT + latitude, 4, stride=NLAT), :]
                out_ref[lat_owner[latitude], part] = rows.astype(bf16)


def circle(quarters_per_turn, numerator, inverse):
    turns = jnp.floor(numerator * inverse + 0.5)
    v = (numerator - turns * quarters_per_turn) * inverse
    z = v * v
    h = math.pi / 2
    sine = v * (h + z * (-(h**3) / 6 + z * (h**5 / 120 + z * (-(h**7) / 5040))))
    cosine = 1.0 + z * (-(h**2) / 2 + z * (h**4 / 24 + z * (-(h**6) / 720 + z * (h**8 / 40320))))
    halves = jnp.floor(turns * 0.5)
    odd_turn = turns - 2.0 * halves
    flip = 1.0 - 2.0 * is_odd(halves)
    swap = odd_turn > 0.5
    out_cos = jnp.where(swap, sine, cosine) * (flip * (1.0 - 2.0 * odd_turn))
    out_sin = jnp.where(swap, cosine, sine) * flip
    return out_cos, -out_sin


def my_points(me_ref, lat_owner, lat_points):
    latitude = jnp.int32(0)
    for index in range(NLAT):
        latitude = jnp.where(lat_owner[index] == me_ref[0], index % NORTH, latitude)
    return lat_points[latitude]


TILES = EIGHTH // LANE
MARGIN = TILES + 1
GROUP = 32
KEPT = 4
STEP = 32


def basis_kernel(
    me_ref, owner_hbm, lat_owner_hbm, lat_points_hbm, after_hbm, near, far_hbm, scale,
    owner, lat_owner, lat_points, waves, far, small, large,
):
    del after_hbm
    copies = [
        pltpu.make_async_copy(owner_hbm, owner, small.at[0]),
        pltpu.make_async_copy(lat_owner_hbm, lat_owner, small.at[1]),
        pltpu.make_async_copy(lat_points_hbm, lat_points, small.at[2]),
    ]
    for copy in copies:
        copy.start()
    for copy in copies:
        copy.wait()
    points = my_points(me_ref, lat_owner, lat_points)
    pair = slot_pairs(jnp.concatenate(owner_rows(owner), axis=1))
    even = jnp.where(is_odd(pair) > 0, TRUNC - pair, pair)
    for index, wave in enumerate((even, TRUNC - even)):
        weight = jnp.where(wave == 0, 1.0, 2.0) * jnp.where(2.0 * wave < points.astype(f32), 1.0, 0.0)
        sign = 1.0 - 2.0 * is_odd(jnp.floor(wave * 0.5))
        scale[2 * index : 2 * index + 1, :] = weight
        scale[2 * index + 1 : 2 * index + 2, :] = weight * sign
        waves[index * PAIRS : (index + 1) * PAIRS, :] = jnp.broadcast_to(to_column(wave), (PAIRS, LANE))
    scale[4:8, :] = jnp.zeros((4, PAIRS), f32)
    quarter = jnp.full((1, LANE), (points // 4).astype(f32))
    inverse = 1.0 / quarter
    column = iota((STEP, LANE), 1).astype(f32)
    outs = []
    for index in range(2):

        def rows_of(block, carry):
            first = pl.multiple_of(block * STEP, STEP)
            wave = waves[pl.ds(index * PAIRS + first, STEP), :]
            cosine, sine = circle(quarter, wave * column, inverse)
            turn_cos, turn_sin = circle(quarter, wave * float(LANE), inverse)
            for tile in range(TILES):
                basis, at = (near, tile) if tile < KEPT else (far, tile - KEPT)
                basis[at, index, pl.ds(first, STEP), :] = cosine.astype(bf16)
                basis[at, index, pl.ds(PAIRS + first, STEP), :] = sine.astype(bf16)
                cosine, sine = cosine * turn_cos - sine * turn_sin, sine * turn_cos + cosine * turn_sin
            return carry

        lax.fori_loop(0, PAIRS // STEP, rows_of, 0)
        for tile in range(TILES - KEPT):
            at = large.at[index * (TILES - KEPT) + tile]
            outs.append(pltpu.make_async_copy(far.at[tile, index], far_hbm.at[tile, index], at))
            outs[-1].start()
    for copy in outs:
        copy.wait()


def fourier_kernel(
    me_ref, lat_owner_hbm, lat_points_hbm, received_ref, scale, near, far_hbm, out_hbm,
    lat_owner, lat_points, far, wide, narrow, left, ahead, back, grid, rounded, small, large,
):
    copies = [
        pltpu.make_async_copy(lat_owner_hbm, lat_owner, small.at[0]),
        pltpu.make_async_copy(lat_points_hbm, lat_points, small.at[1]),
    ]
    pieces = [pltpu.make_async_copy(far_hbm.at[tile], far.at[tile], large.at[tile]) for tile in range(TILES - KEPT)]
    for copy in copies + pieces:
        copy.start()
    grid[...] = jnp.zeros(grid.shape, f32)
    for source in range(N_WAVE):
        for part in range(SLOTS // 4):
            wide[pl.ds(source * 24 + 4 * part, 4), :] = received_ref[source, part].astype(f32)
    for index in range(2):
        for pair in range(PAIRS_DEV):
            slot = index * PAIRS_DEV + pair
            rows = wide[pl.ds(2 * pair + index, N_WAVE, stride=24), :]
            narrow[slot * N_WAVE : (slot + 1) * N_WAVE, :] = rows.astype(bf16)
    out_row, in_col = iota((COLS, COLS), 0), iota((COLS, COLS), 1)
    turn = jnp.where(in_col == 2 * (out_row % LEVELS) + out_row // LEVELS, 1.0, 0.0).astype(bf16)
    for index in range(2):
        turned = lax.dot_general(
            turn,
            narrow[index * PAIRS : (index + 1) * PAIRS, :],
            (((1,), (1,)), ((), ())),
            preferred_element_type=f32,
        )
        weighted = turned * scale[2 * index : 2 * index + 1, :]
        signed = turned * scale[2 * index + 1 : 2 * index + 2, :]
        left[index, 0, :LEVELS] = weighted[:LEVELS].astype(bf16)
        left[index, 1, :LEVELS] = weighted[LEVELS:].astype(bf16)
        if index == 0:
            left[index, 0, LEVELS:] = signed[:LEVELS].astype(bf16)
            left[index, 1, LEVELS:] = signed[LEVELS:].astype(bf16)
        else:
            left[index, 0, LEVELS:] = signed[LEVELS:].astype(bf16)
            left[index, 1, LEVELS:] = -signed[:LEVELS].astype(bf16)
    for copy in copies:
        copy.wait()
    quarter = my_points(me_ref, lat_owner, lat_points) // 4
    half = quarter // 2
    for first in range(0, EIGHTH, 2 * LANE):
        at = slice(first, first + 2 * LANE)
        tiles = range(first // LANE, first // LANE + 2)
        if tiles.start == KEPT:
            for piece in pieces:
                piece.wait()
        sums = []
        for index in range(2):
            right = jnp.concatenate(
                [near[tile, index] if tile < KEPT else far[tile - KEPT, index] for tile in tiles], axis=1
            )
            sums.append(jnp.dot(left[index, 0], right[:PAIRS], preferred_element_type=f32))
            sums.append(jnp.dot(left[index, 1], right[PAIRS:], preferred_element_type=f32))
        even_cos, even_sin, odd_cos, odd_sin = sums
        even, odd = even_cos + even_sin, odd_cos + odd_sin
        ahead[0, :, at] = even[:LEVELS] + odd[:LEVELS]
        ahead[1, :, at] = even[LEVELS:] - odd[LEVELS:]
        ahead[2, :, at] = even[:LEVELS] - odd[:LEVELS]
        ahead[3, :, at] = even[LEVELS:] + odd[LEVELS:]
        even, odd = even_cos - even_sin, odd_cos - odd_sin
        back[0, :, at] = even[LEVELS:] - odd[LEVELS:]
        back[1, :, at] = even[:LEVELS] - odd[:LEVELS]
        back[2, :, at] = even[LEVELS:] + odd[LEVELS:]
        back[3, :, at] = even[:LEVELS] + odd[:LEVELS]
    lane = iota((GROUP, LANE), 1)
    zero = jnp.zeros((GROUP, LANE), f32)
    outs = []
    for group in range(LEVELS // GROUP):
        rows = slice(group * GROUP, (group + 1) * GROUP)

        def put(tile, value, first, last):
            at = pl.ds(pl.multiple_of((tile + MARGIN) * LANE, LANE), LANE)
            point = lane + tile * LANE
            pltpu.store(grid.at[rows, at], value, mask=(point >= first) & (point <= last))

        for index in range(4):
            offset = index * quarter
            shift = offset % LANE
            before = zero
            for tile in range(TILES + (1 if index else 0)):
                now = zero
                if tile < TILES:
                    now = ahead[index, rows, tile * LANE : (tile + 1) * LANE]
                    if index:
                        now = pltpu.roll(now, shift, 1)
                value = jnp.where(lane < shift, before, now) if index else now
                put(offset // LANE + tile, value, offset, offset + half)
                before = now
            offset = (index + 1) * quarter
            shift = offset % LANE
            order = lax.rem(shift - lane + LANE, LANE)
            before = zero
            for tile in range(TILES + 1):
                now = zero
                if tile < TILES:
                    now = jnp.take_along_axis(
                        back[index, rows, tile * LANE : (tile + 1) * LANE], order, axis=1, mode="promise_in_bounds"
                    )
                value = jnp.where(lane <= shift, now, before)
                put(offset // LANE - tile, value, index * quarter + half + 1, offset - 1)
                before = now
        rounded[rows, :] = grid[rows, MARGIN * LANE :].astype(bf16)
        at = pl.ds(group * GROUP, GROUP)
        outs.append(pltpu.make_async_copy(rounded.at[at], out_hbm.at[0, at], small.at[2 + group]))
        outs[-1].start()
    for copy in outs:
        copy.wait()


def params(mib):
    return pltpu.CompilerParams(vmem_limit_bytes=mib * 1024 * 1024)


def per_device(spectral, table, wave_owner, lat_owner, lat_points):
    me = lax.axis_index("wave").astype(jnp.int32).reshape(1)
    waves = wave_owner.shape[0]
    tables = lax.all_gather(table, "lev", axis=0, tiled=False)
    spectral, wave_owner, lat_owner, lat_points = [
        pltpu.with_memory_space_constraint(array, pltpu.HBM)
        for array in (spectral, wave_owner, lat_owner, lat_points)
    ]
    owner_scratch = pltpu.VMEM((waves,), jnp.int32)
    lat_owner_scratch = pltpu.SMEM((NLAT,), jnp.int32)
    lat_points_scratch = pltpu.SMEM((NORTH,), jnp.int32)
    dma = pltpu.SemaphoreType.DMA
    four = pl.pallas_call(
        legendre_kernel,
        out_shape=jax.ShapeDtypeStruct((N_WAVE, SLOTS // 4, 4, COLS), bf16),
        in_specs=[SMEM, HBM, HBM, VMEM, HBM],
        out_specs=VMEM,
        scratch_shapes=[
            owner_scratch,
            lat_owner_scratch,
            pltpu.VMEM((NORTH, ROWS_PAD), f32),
            pltpu.VMEM((ROWS_DEV, COLS), bf16),
            pltpu.VMEM((SLOTS * NLAT, COLS), f32),
            dma((2,)),
            dma((len(PIECES),)),
        ],
        compiler_params=params(24),
        name="legendre",
    )(me, wave_owner, lat_owner, tables, spectral)
    received = lax.all_to_all(four, "wave", split_axis=0, concat_axis=0, tiled=True)
    near_shape = (KEPT, 2, 2 * PAIRS, LANE)
    far_shape = (TILES - KEPT, 2, 2 * PAIRS, LANE)
    near, far, scale = pl.pallas_call(
        basis_kernel,
        out_shape=(pltpu.VMEM(near_shape, bf16), pltpu.HBM(far_shape, bf16), pltpu.VMEM((8, PAIRS), f32)),
        in_specs=[SMEM, HBM, HBM, HBM, HBM],
        out_specs=(VMEM, HBM, VMEM),
        scratch_shapes=[
            owner_scratch,
            lat_owner_scratch,
            lat_points_scratch,
            pltpu.VMEM((2 * PAIRS, LANE), f32),
            pltpu.VMEM(far_shape, bf16),
            dma((3,)),
            dma((2 * (TILES - KEPT),)),
        ],
        compiler_params=params(16),
        name="basis",
    )(me, wave_owner, lat_owner, lat_points, pltpu.with_memory_space_constraint(four, pltpu.HBM))
    return pl.pallas_call(
        fourier_kernel,
        out_shape=pltpu.HBM((1, LEVELS, NLON_PAD), bf16),
        in_specs=[SMEM, HBM, HBM, VMEM, VMEM, VMEM, HBM],
        out_specs=HBM,
        scratch_shapes=[
            lat_owner_scratch,
            lat_points_scratch,
            pltpu.VMEM(far_shape, bf16),
            pltpu.VMEM((N_WAVE * 24, COLS), f32),
            pltpu.VMEM((SLOTS * N_WAVE, COLS), bf16),
            pltpu.VMEM((2, 2, COLS, PAIRS), bf16),
            pltpu.VMEM((4, LEVELS, EIGHTH), f32),
            pltpu.VMEM((4, LEVELS, EIGHTH), f32),
            pltpu.VMEM((LEVELS, MARGIN * LANE + NLON_PAD), f32),
            pltpu.VMEM((LEVELS, NLON_PAD), bf16),
            dma((2 + LEVELS // GROUP,)),
            dma((TILES - KEPT,)),
        ],
        compiler_params=params(24),
        name="fourier",
    )(
        me,
        lat_owner,
        lat_points,
        received,
        pltpu.with_memory_space_constraint(scale, pltpu.VMEM),
        pltpu.with_memory_space_constraint(near, pltpu.VMEM),
        pltpu.with_memory_space_constraint(far, pltpu.HBM),
    )


def solution(mesh):
    in_specs = (P("wave", "lev"), P("lev", "wave"), P(), P(), P())
    out_specs = P("wave", "lev", None)
    return jax.shard_map(
        per_device, mesh=mesh, in_specs=in_specs, out_specs=out_specs, check_vma=False
    )
```

```python
import math

import jax
import jax.numpy as jnp
from jax import lax
from jax.experimental import pallas as pl
from jax.experimental.pallas import tpu as pltpu
from jax.sharding import PartitionSpec as P

TRUNC = 1279
PAIRS = 640
PAIRS_DEV = 10
PAIR_ROWS = 1282
ROWS_DEV = 12820
ROWS_PAD = 12928
N_WAVE = 64
NLAT = 64
NORTH = 32
LEVELS = 64
COLS = 128
SLOTS = 20
EIGHTH = 768
NLON_PAD = 5376
LANE = 128

VMEM = pl.BlockSpec(memory_space=pltpu.VMEM)
SMEM = pl.BlockSpec(memory_space=pltpu.SMEM)
HBM = pl.BlockSpec(memory_space=pltpu.HBM)
f32 = jnp.float32
bf16 = jnp.bfloat16


def iota(shape, dim):
    return lax.broadcasted_iota(jnp.int32, shape, dim)


def to_column(row):
    eye = iota((LANE, LANE), 0) == iota((LANE, LANE), 1)
    parts = []
    for first in range(0, row.shape[1], LANE):
        block = jnp.broadcast_to(row[:, first : first + LANE], (LANE, LANE))
        parts.append(jnp.sum(jnp.where(eye, block, 0.0), axis=1, keepdims=True))
    return jnp.concatenate(parts, axis=0)


def slot_pairs(owner_row):
    owner_col = to_column(owner_row)
    pair_row = iota((1, PAIRS), 1)
    rank = jnp.zeros((1, PAIRS), f32)
    for first in range(0, PAIRS, LANE):
        same = owner_col[first : first + LANE] == owner_row
        earlier = (iota((LANE, PAIRS), 0) + first) < pair_row
        rank += jnp.sum(jnp.where(same & earlier, 1.0, 0.0), axis=0, keepdims=True)
    slot_col = to_column(rank * N_WAVE + owner_row)
    slot_row = iota((1, PAIRS), 1).astype(f32)
    pairs = jnp.zeros((1, PAIRS), f32)
    for first in range(0, PAIRS, LANE):
        here = slot_col[first : first + LANE] == slot_row
        pair = (iota((LANE, PAIRS), 0) + first).astype(f32)
        pairs += jnp.sum(jnp.where(here, pair, 0.0), axis=0, keepdims=True)
    return pairs


def is_odd(value):
    return value - 2.0 * jnp.floor(value * 0.5)


def owner_rows(owner_ref):
    return [owner_ref[pl.ds(first, LANE)].reshape(1, LANE).astype(f32) for first in range(0, PAIRS, LANE)]


def local_pairs(rows, me):
    count = len(rows)
    own = jnp.concatenate([jnp.where(row == me, 1.0, 0.0) for row in rows], axis=0)
    pair = (iota((count, LANE), 0) * LANE + iota((count, LANE), 1)).astype(f32)
    before = jnp.where(iota((LANE, LANE), 0) < iota((LANE, LANE), 1), 1.0, 0.0).astype(bf16)
    rank = jnp.dot(own.astype(bf16), before, preferred_element_type=f32)
    totals = jnp.sum(own, axis=1, keepdims=True)
    carry = jnp.zeros((1, 1), f32)
    carries = []
    for index in range(count):
        carries.append(carry)
        carry = carry + totals[index : index + 1]
    rank = jnp.where(own > 0, rank + jnp.concatenate(carries, axis=0), -1.0)
    return [
        jnp.sum(jnp.sum(jnp.where(rank == index, pair, 0.0), axis=1, keepdims=True), axis=0, keepdims=True)
        for index in range(PAIRS_DEV)
    ]


def first_row(pair):
    return PAIR_ROWS * pair // LANE * LANE


def last_row(pair):
    return min(-(-PAIR_ROWS * (pair + 1) // LANE) * LANE, ROWS_DEV)


def legendre_kernel(
    me_ref, owner_hbm, lat_owner_hbm, table_ref, spectral_hbm, out_ref, owner, lat_owner, table, spectral, four, small, large
):
    copies = [
        pltpu.make_async_copy(owner_hbm, owner, small.at[0]),
        pltpu.make_async_copy(lat_owner_hbm, lat_owner, small.at[1]),
    ]
    whole = pltpu.make_async_copy(spectral_hbm, spectral, large.at[0])
    for copy in [whole] + copies:
        copy.start()
    for index in range(8):
        table[4 * index : 4 * index + 4, 0:ROWS_DEV] = table_ref[index].astype(f32)
    for copy in copies:
        copy.wait()
    locals_ = local_pairs(owner_rows(owner), me_ref[0].astype(f32))
    for pair in range(PAIRS_DEV):
        start, stop = first_row(pair), last_row(pair)
        width = stop - start
        row = (iota((1, width), 1) + (start - PAIR_ROWS * pair)).astype(f32)
        q = locals_[pair]
        q_odd = is_odd(q)
        split = TRUNC + 1 - q
        low = jnp.where((row >= 0) & (row < split), 1.0, 0.0)
        high = jnp.where((row >= split) & (row < TRUNC + 2), 1.0, 0.0)
        even = jnp.where(q_odd > 0, high, low)
        odd = low + high - even
        odd_sign = 1.0 - 2.0 * is_odd(row)
        even_sign = odd_sign * (1.0 - 2.0 * q_odd)
        block = table[:, start:stop].astype(bf16)
        left = jnp.concatenate(
            [block * mask.astype(bf16) for mask in (even, even * even_sign, odd, odd * odd_sign)], axis=0
        )
        if pair == 0:
            whole.wait()
        values = jnp.dot(left, spectral[start:stop, :], preferred_element_type=f32)
        four[2 * pair * NLAT : 2 * (pair + 1) * NLAT, :] = values
        if pair % 2 == 1:
            part = pair // 2
            for latitude in range(NLAT):
                rows = four[pl.ds(4 * part * NLAT + latitude, 4, stride=NLAT), :]
                out_ref[lat_owner[latitude], part] = rows.astype(bf16)


def circle(quarters_per_turn, numerator, inverse):
    turns = jnp.floor(numerator * inverse + 0.5)
    v = (numerator - turns * quarters_per_turn) * inverse
    z = v * v
    h = math.pi / 2
    sine = v * (h + z * (-(h**3) / 6 + z * (h**5 / 120 + z * (-(h**7) / 5040))))
    cosine = 1.0 + z * (-(h**2) / 2 + z * (h**4 / 24 + z * (-(h**6) / 720 + z * (h**8 / 40320))))
    halves = jnp.floor(turns * 0.5)
    odd_turn = turns - 2.0 * halves
    flip = 1.0 - 2.0 * is_odd(halves)
    swap = odd_turn > 0.5
    out_cos = jnp.where(swap, sine, cosine) * (flip * (1.0 - 2.0 * odd_turn))
    out_sin = jnp.where(swap, cosine, sine) * flip
    return out_cos, -out_sin


def my_points(me_ref, lat_owner, lat_points):
    latitude = jnp.int32(0)
    for index in range(NLAT):
        latitude = jnp.where(lat_owner[index] == me_ref[0], index % NORTH, latitude)
    return lat_points[latitude]


TILES = EIGHTH // LANE
MARGIN = TILES + 1
GROUP = 32
KEPT = 4
STEP = 32


def basis_kernel(
    me_ref, owner_hbm, lat_owner_hbm, lat_points_hbm, after_hbm, near, far_hbm, scale,
    owner, lat_owner, lat_points, waves, far, small, large,
):
    del after_hbm
    copies = [
        pltpu.make_async_copy(owner_hbm, owner, small.at[0]),
        pltpu.make_async_copy(lat_owner_hbm, lat_owner, small.at[1]),
        pltpu.make_async_copy(lat_points_hbm, lat_points, small.at[2]),
    ]
    for copy in copies:
        copy.start()
    for copy in copies:
        copy.wait()
    points = my_points(me_ref, lat_owner, lat_points)
    pair = slot_pairs(jnp.concatenate(owner_rows(owner), axis=1))
    even = jnp.where(is_odd(pair) > 0, TRUNC - pair, pair)
    for index, wave in enumerate((even, TRUNC - even)):
        weight = jnp.where(wave == 0, 1.0, 2.0) * jnp.where(2.0 * wave < points.astype(f32), 1.0, 0.0)
        sign = 1.0 - 2.0 * is_odd(jnp.floor(wave * 0.5))
        scale[2 * index : 2 * index + 1, :] = weight
        scale[2 * index + 1 : 2 * index + 2, :] = weight * sign
        waves[index * PAIRS : (index + 1) * PAIRS, :] = jnp.broadcast_to(to_column(wave), (PAIRS, LANE))
    scale[4:8, :] = jnp.zeros((4, PAIRS), f32)
    quarter = jnp.full((1, LANE), (points // 4).astype(f32))
    inverse = 1.0 / quarter
    column = iota((STEP, LANE), 1).astype(f32)
    outs = []
    for index in range(2):

        def rows_of(block, carry):
            first = pl.multiple_of(block * STEP, STEP)
            wave = waves[pl.ds(index * PAIRS + first, STEP), :]
            cosine, sine = circle(quarter, wave * column, inverse)
            turn_cos, turn_sin = circle(quarter, wave * float(LANE), inverse)
            for tile in range(TILES):
                basis, at = (near, tile) if tile < KEPT else (far, tile - KEPT)
                basis[at, index, pl.ds(first, STEP), :] = cosine.astype(bf16)
                basis[at, index, pl.ds(PAIRS + first, STEP), :] = sine.astype(bf16)
                cosine, sine = cosine * turn_cos - sine * turn_sin, sine * turn_cos + cosine * turn_sin
            return carry

        lax.fori_loop(0, PAIRS // STEP, rows_of, 0)
        for tile in range(TILES - KEPT):
            at = large.at[index * (TILES - KEPT) + tile]
            outs.append(pltpu.make_async_copy(far.at[tile, index], far_hbm.at[tile, index], at))
            outs[-1].start()
    for copy in outs:
        copy.wait()


def fourier_kernel(
    me_ref, lat_owner_hbm, lat_points_hbm, received_ref, scale, near, far_hbm, out_hbm,
    lat_owner, lat_points, far, wide, narrow, left, ahead, back, grid, rounded, small, large,
):
    copies = [
        pltpu.make_async_copy(lat_owner_hbm, lat_owner, small.at[0]),
        pltpu.make_async_copy(lat_points_hbm, lat_points, small.at[1]),
    ]
    pieces = [pltpu.make_async_copy(far_hbm.at[tile], far.at[tile], large.at[tile]) for tile in range(TILES - KEPT)]
    for copy in copies + pieces:
        copy.start()
    grid[...] = jnp.zeros(grid.shape, f32)
    for source in range(N_WAVE):
        for part in range(SLOTS // 4):
            wide[pl.ds(source * 24 + 4 * part, 4), :] = received_ref[source, part].astype(f32)
    for index in range(2):
        for pair in range(PAIRS_DEV):
            slot = index * PAIRS_DEV + pair
            rows = wide[pl.ds(2 * pair + index, N_WAVE, stride=24), :]
            narrow[slot * N_WAVE : (slot + 1) * N_WAVE, :] = rows.astype(bf16)
    out_row, in_col = iota((COLS, COLS), 0), iota((COLS, COLS), 1)
    turn = jnp.where(in_col == 2 * (out_row % LEVELS) + out_row // LEVELS, 1.0, 0.0).astype(bf16)
    for index in range(2):
        turned = lax.dot_general(
            turn,
            narrow[index * PAIRS : (index + 1) * PAIRS, :],
            (((1,), (1,)), ((), ())),
            preferred_element_type=f32,
        )
        weighted = turned * scale[2 * index : 2 * index + 1, :]
        signed = turned * scale[2 * index + 1 : 2 * index + 2, :]
        left[index, 0, :LEVELS] = weighted[:LEVELS].astype(bf16)
        left[index, 1, :LEVELS] = weighted[LEVELS:].astype(bf16)
        if index == 0:
            left[index, 0, LEVELS:] = signed[:LEVELS].astype(bf16)
            left[index, 1, LEVELS:] = signed[LEVELS:].astype(bf16)
        else:
            left[index, 0, LEVELS:] = signed[LEVELS:].astype(bf16)
            left[index, 1, LEVELS:] = -signed[:LEVELS].astype(bf16)
    for copy in copies:
        copy.wait()
    quarter = my_points(me_ref, lat_owner, lat_points) // 4
    half = quarter // 2
    for first in range(0, EIGHTH, 2 * LANE):
        at = slice(first, first + 2 * LANE)
        tiles = range(first // LANE, first // LANE + 2)
        if tiles.start == KEPT:
            for piece in pieces:
                piece.wait()
        sums = []
        for index in range(2):
            right = jnp.concatenate(
                [near[tile, index] if tile < KEPT else far[tile - KEPT, index] for tile in tiles], axis=1
            )
            sums.append(jnp.dot(left[index, 0], right[:PAIRS], preferred_element_type=f32))
            sums.append(jnp.dot(left[index, 1], right[PAIRS:], preferred_element_type=f32))
        even_cos, even_sin, odd_cos, odd_sin = sums
        even, odd = even_cos + even_sin, odd_cos + odd_sin
        ahead[0, :, at] = even[:LEVELS] + odd[:LEVELS]
        ahead[1, :, at] = even[LEVELS:] - odd[LEVELS:]
        ahead[2, :, at] = even[:LEVELS] - odd[:LEVELS]
        ahead[3, :, at] = even[LEVELS:] + odd[LEVELS:]
        even, odd = even_cos - even_sin, odd_cos - odd_sin
        back[0, :, at] = even[LEVELS:] - odd[LEVELS:]
        back[1, :, at] = even[:LEVELS] - odd[:LEVELS]
        back[2, :, at] = even[LEVELS:] + odd[LEVELS:]
        back[3, :, at] = even[:LEVELS] + odd[:LEVELS]
    lane = iota((GROUP, LANE), 1)
    zero = jnp.zeros((GROUP, LANE), f32)
    outs = []
    for group in range(LEVELS // GROUP):
        rows = slice(group * GROUP, (group + 1) * GROUP)

        def put(tile, value, first, last):
            at = pl.ds(pl.multiple_of((tile + MARGIN) * LANE, LANE), LANE)
            point = lane + tile * LANE
            pltpu.store(grid.at[rows, at], value, mask=(point >= first) & (point <= last))

        for index in range(4):
            offset = index * quarter
            shift = offset % LANE
            before = zero
            for tile in range(TILES + (1 if index else 0)):
                now = zero
                if tile < TILES:
                    now = ahead[index, rows, tile * LANE : (tile + 1) * LANE]
                    if index:
                        now = pltpu.roll(now, shift, 1)
                value = jnp.where(lane < shift, before, now) if index else now
                put(offset // LANE + tile, value, offset, offset + half)
                before = now
            offset = (index + 1) * quarter
            shift = offset % LANE
            order = lax.rem(shift - lane + LANE, LANE)
            before = zero
            for tile in range(TILES + 1):
                now = zero
                if tile < TILES:
                    now = jnp.take_along_axis(
                        back[index, rows, tile * LANE : (tile + 1) * LANE], order, axis=1, mode="promise_in_bounds"
                    )
                value = jnp.where(lane <= shift, now, before)
                put(offset // LANE - tile, value, index * quarter + half + 1, offset - 1)
                before = now
        rounded[rows, :] = grid[rows, MARGIN * LANE :].astype(bf16)
        at = pl.ds(group * GROUP, GROUP)
        outs.append(pltpu.make_async_copy(rounded.at[at], out_hbm.at[0, at], small.at[2 + group]))
        outs[-1].start()
    for copy in outs:
        copy.wait()


def params(mib):
    return pltpu.CompilerParams(vmem_limit_bytes=mib * 1024 * 1024)


def per_device(spectral, table, wave_owner, lat_owner, lat_points):
    me = lax.axis_index("wave").astype(jnp.int32).reshape(1)
    waves = wave_owner.shape[0]
    tables = lax.all_gather(table, "lev", axis=0, tiled=False)
    spectral, wave_owner, lat_owner, lat_points = [
        pltpu.with_memory_space_constraint(array, pltpu.HBM)
        for array in (spectral, wave_owner, lat_owner, lat_points)
    ]
    owner_scratch = pltpu.VMEM((waves,), jnp.int32)
    lat_owner_scratch = pltpu.SMEM((NLAT,), jnp.int32)
    lat_points_scratch = pltpu.SMEM((NORTH,), jnp.int32)
    dma = pltpu.SemaphoreType.DMA
    four = pl.pallas_call(
        legendre_kernel,
        out_shape=jax.ShapeDtypeStruct((N_WAVE, SLOTS // 4, 4, COLS), bf16),
        in_specs=[SMEM, HBM, HBM, VMEM, HBM],
        out_specs=VMEM,
        scratch_shapes=[
            owner_scratch,
            lat_owner_scratch,
            pltpu.VMEM((NORTH, ROWS_PAD), f32),
            pltpu.VMEM((ROWS_DEV, COLS), bf16),
            pltpu.VMEM((SLOTS * NLAT, COLS), f32),
            dma((2,)),
            dma((1,)),
        ],
        compiler_params=params(24),
        name="legendre",
    )(me, wave_owner, lat_owner, tables, spectral)
    received = lax.all_to_all(four, "wave", split_axis=0, concat_axis=0, tiled=True)
    near_shape = (KEPT, 2, 2 * PAIRS, LANE)
    far_shape = (TILES - KEPT, 2, 2 * PAIRS, LANE)
    near, far, scale = pl.pallas_call(
        basis_kernel,
        out_shape=(pltpu.VMEM(near_shape, bf16), pltpu.HBM(far_shape, bf16), pltpu.VMEM((8, PAIRS), f32)),
        in_specs=[SMEM, HBM, HBM, HBM, HBM],
        out_specs=(VMEM, HBM, VMEM),
        scratch_shapes=[
            owner_scratch,
            lat_owner_scratch,
            lat_points_scratch,
            pltpu.VMEM((2 * PAIRS, LANE), f32),
            pltpu.VMEM(far_shape, bf16),
            dma((3,)),
            dma((2 * (TILES - KEPT),)),
        ],
        compiler_params=params(16),
        name="basis",
    )(me, wave_owner, lat_owner, lat_points, pltpu.with_memory_space_constraint(four, pltpu.HBM))
    return pl.pallas_call(
        fourier_kernel,
        out_shape=pltpu.HBM((1, LEVELS, NLON_PAD), bf16),
        in_specs=[SMEM, HBM, HBM, VMEM, VMEM, VMEM, HBM],
        out_specs=HBM,
        scratch_shapes=[
            lat_owner_scratch,
            lat_points_scratch,
            pltpu.VMEM(far_shape, bf16),
            pltpu.VMEM((N_WAVE * 24, COLS), f32),
            pltpu.VMEM((SLOTS * N_WAVE, COLS), bf16),
            pltpu.VMEM((2, 2, COLS, PAIRS), bf16),
            pltpu.VMEM((4, LEVELS, EIGHTH), f32),
            pltpu.VMEM((4, LEVELS, EIGHTH), f32),
            pltpu.VMEM((LEVELS, MARGIN * LANE + NLON_PAD), f32),
            pltpu.VMEM((LEVELS, NLON_PAD), bf16),
            dma((2 + LEVELS // GROUP,)),
            dma((TILES - KEPT,)),
        ],
        compiler_params=params(24),
        name="fourier",
    )(
        me,
        lat_owner,
        lat_points,
        received,
        pltpu.with_memory_space_constraint(scale, pltpu.VMEM),
        pltpu.with_memory_space_constraint(near, pltpu.VMEM),
        pltpu.with_memory_space_constraint(far, pltpu.HBM),
    )


def solution(mesh):
    in_specs = (P("wave", "lev"), P("lev", "wave"), P(), P(), P())
    out_specs = P("wave", "lev", None)
    return jax.shard_map(
        per_device, mesh=mesh, in_specs=in_specs, out_specs=out_specs, check_vma=False
    )
```

```python
import math

import jax
import jax.numpy as jnp
from jax import lax
from jax.experimental import pallas as pl
from jax.experimental.pallas import tpu as pltpu
from jax.sharding import PartitionSpec as P

TRUNC = 1279
PAIRS = 640
PAIRS_DEV = 10
PAIR_ROWS = 1282
ROWS_DEV = 12820
ROWS_PAD = 12928
N_WAVE = 64
NLAT = 64
NORTH = 32
LEVELS = 64
COLS = 128
SLOTS = 20
EIGHTH = 768
NLON_PAD = 5376
LANE = 128

VMEM = pl.BlockSpec(memory_space=pltpu.VMEM)
SMEM = pl.BlockSpec(memory_space=pltpu.SMEM)
HBM = pl.BlockSpec(memory_space=pltpu.HBM)
f32 = jnp.float32
bf16 = jnp.bfloat16


def iota(shape, dim):
    return lax.broadcasted_iota(jnp.int32, shape, dim)


def to_column(row):
    eye = iota((LANE, LANE), 0) == iota((LANE, LANE), 1)
    parts = []
    for first in range(0, row.shape[1], LANE):
        block = jnp.broadcast_to(row[:, first : first + LANE], (LANE, LANE))
        parts.append(jnp.sum(jnp.where(eye, block, 0.0), axis=1, keepdims=True))
    return jnp.concatenate(parts, axis=0)


def slot_pairs(owner_row):
    owner_col = to_column(owner_row)
    pair_row = iota((1, PAIRS), 1)
    rank = jnp.zeros((1, PAIRS), f32)
    for first in range(0, PAIRS, LANE):
        same = owner_col[first : first + LANE] == owner_row
        earlier = (iota((LANE, PAIRS), 0) + first) < pair_row
        rank += jnp.sum(jnp.where(same & earlier, 1.0, 0.0), axis=0, keepdims=True)
    slot_col = to_column(rank * N_WAVE + owner_row)
    slot_row = iota((1, PAIRS), 1).astype(f32)
    pairs = jnp.zeros((1, PAIRS), f32)
    for first in range(0, PAIRS, LANE):
        here = slot_col[first : first + LANE] == slot_row
        pair = (iota((LANE, PAIRS), 0) + first).astype(f32)
        pairs += jnp.sum(jnp.where(here, pair, 0.0), axis=0, keepdims=True)
    return pairs


def is_odd(value):
    return value - 2.0 * jnp.floor(value * 0.5)


def owner_rows(owner_ref):
    return [owner_ref[pl.ds(first, LANE)].reshape(1, LANE).astype(f32) for first in range(0, PAIRS, LANE)]


def local_pairs(rows, me):
    count = len(rows)
    own = jnp.concatenate([jnp.where(row == me, 1.0, 0.0) for row in rows], axis=0)
    pair = (iota((count, LANE), 0) * LANE + iota((count, LANE), 1)).astype(f32)
    before = jnp.where(iota((LANE, LANE), 0) < iota((LANE, LANE), 1), 1.0, 0.0).astype(bf16)
    rank = jnp.dot(own.astype(bf16), before, preferred_element_type=f32)
    totals = jnp.sum(own, axis=1, keepdims=True)
    carry = jnp.zeros((1, 1), f32)
    carries = []
    for index in range(count):
        carries.append(carry)
        carry = carry + totals[index : index + 1]
    rank = jnp.where(own > 0, rank + jnp.concatenate(carries, axis=0), -1.0)
    return [
        jnp.sum(jnp.sum(jnp.where(rank == index, pair, 0.0), axis=1, keepdims=True), axis=0, keepdims=True)
        for index in range(PAIRS_DEV)
    ]


def first_row(pair):
    return PAIR_ROWS * pair // LANE * LANE


def last_row(pair):
    return min(-(-PAIR_ROWS * (pair + 1) // LANE) * LANE, ROWS_DEV)


PIECES = (0, 2, 5)


def legendre_kernel(
    me_ref, owner_hbm, lat_owner_hbm, table_ref, spectral_hbm, out_hbm,
    owner, lat_owner, table, spectral, four, parts, small, large, leave,
):
    copies = [
        pltpu.make_async_copy(owner_hbm, owner, small.at[0]),
        pltpu.make_async_copy(lat_owner_hbm, lat_owner, small.at[1]),
    ]
    pieces = {}
    for index, (pair, end) in enumerate(zip(PIECES, PIECES[1:] + (PAIRS_DEV,))):
        start = last_row(pair - 1) if pair else 0
        at = pl.ds(start, last_row(end - 1) - start)
        pieces[pair] = pltpu.make_async_copy(spectral_hbm.at[at], spectral.at[at], large.at[index])
    for copy in copies + list(pieces.values()):
        copy.start()
    for index in range(8):
        table[4 * index : 4 * index + 4, 0:ROWS_DEV] = table_ref[index].astype(f32)
    for copy in copies:
        copy.wait()
    locals_ = local_pairs(owner_rows(owner), me_ref[0].astype(f32))
    outs = []
    for pair in range(PAIRS_DEV):
        start, stop = first_row(pair), last_row(pair)
        width = stop - start
        row = (iota((1, width), 1) + (start - PAIR_ROWS * pair)).astype(f32)
        q = locals_[pair]
        q_odd = is_odd(q)
        split = TRUNC + 1 - q
        low = jnp.where((row >= 0) & (row < split), 1.0, 0.0)
        high = jnp.where((row >= split) & (row < TRUNC + 2), 1.0, 0.0)
        even = jnp.where(q_odd > 0, high, low)
        odd = low + high - even
        odd_sign = 1.0 - 2.0 * is_odd(row)
        even_sign = odd_sign * (1.0 - 2.0 * q_odd)
        block = table[:, start:stop].astype(bf16)
        left = jnp.concatenate(
            [block * mask.astype(bf16) for mask in (even, even * even_sign, odd, odd * odd_sign)], axis=0
        )
        if pair in pieces:
            pieces[pair].wait()
        values = jnp.dot(left, spectral[start:stop, :], preferred_element_type=f32)
        four[2 * pair * NLAT : 2 * (pair + 1) * NLAT, :] = values
        if pair % 2 == 1:
            part = pair // 2
            for latitude in range(NLAT):
                rows = four[pl.ds(4 * part * NLAT + latitude, 4, stride=NLAT), :]
                parts[part, lat_owner[latitude]] = rows.astype(bf16)
            outs.append(pltpu.make_async_copy(parts.at[part], out_hbm.at[:, part], leave.at[part]))
            outs[-1].start()
    for copy in outs:
        copy.wait()


def circle(quarters_per_turn, numerator, inverse):
    turns = jnp.floor(numerator * inverse + 0.5)
    v = (numerator - turns * quarters_per_turn) * inverse
    z = v * v
    h = math.pi / 2
    sine = v * (h + z * (-(h**3) / 6 + z * (h**5 / 120 + z * (-(h**7) / 5040))))
    cosine = 1.0 + z * (-(h**2) / 2 + z * (h**4 / 24 + z * (-(h**6) / 720 + z * (h**8 / 40320))))
    halves = jnp.floor(turns * 0.5)
    odd_turn = turns - 2.0 * halves
    flip = 1.0 - 2.0 * is_odd(halves)
    swap = odd_turn > 0.5
    out_cos = jnp.where(swap, sine, cosine) * (flip * (1.0 - 2.0 * odd_turn))
    out_sin = jnp.where(swap, cosine, sine) * flip
    return out_cos, -out_sin


def my_points(me_ref, lat_owner, lat_points):
    latitude = jnp.int32(0)
    for index in range(NLAT):
        latitude = jnp.where(lat_owner[index] == me_ref[0], index % NORTH, latitude)
    return lat_points[latitude]


TILES = EIGHTH // LANE
MARGIN = TILES + 1
GROUP = 32
KEPT = 4
STEP = 32


def basis_kernel(
    me_ref, owner_hbm, lat_owner_hbm, lat_points_hbm, after_hbm, near, far_hbm, scale,
    owner, lat_owner, lat_points, waves, far, small, large,
):
    del after_hbm
    copies = [
        pltpu.make_async_copy(owner_hbm, owner, small.at[0]),
        pltpu.make_async_copy(lat_owner_hbm, lat_owner, small.at[1]),
        pltpu.make_async_copy(lat_points_hbm, lat_points, small.at[2]),
    ]
    for copy in copies:
        copy.start()
    for copy in copies:
        copy.wait()
    points = my_points(me_ref, lat_owner, lat_points)
    pair = slot_pairs(jnp.concatenate(owner_rows(owner), axis=1))
    even = jnp.where(is_odd(pair) > 0, TRUNC - pair, pair)
    for index, wave in enumerate((even, TRUNC - even)):
        weight = jnp.where(wave == 0, 1.0, 2.0) * jnp.where(2.0 * wave < points.astype(f32), 1.0, 0.0)
        sign = 1.0 - 2.0 * is_odd(jnp.floor(wave * 0.5))
        scale[2 * index : 2 * index + 1, :] = weight
        scale[2 * index + 1 : 2 * index + 2, :] = weight * sign
        waves[index * PAIRS : (index + 1) * PAIRS, :] = jnp.broadcast_to(to_column(wave), (PAIRS, LANE))
    scale[4:8, :] = jnp.zeros((4, PAIRS), f32)
    quarter = jnp.full((1, LANE), (points // 4).astype(f32))
    inverse = 1.0 / quarter
    column = iota((STEP, LANE), 1).astype(f32)
    outs = []
    for index in range(2):

        def rows_of(block, carry):
            first = pl.multiple_of(block * STEP, STEP)
            wave = waves[pl.ds(index * PAIRS + first, STEP), :]
            cosine, sine = circle(quarter, wave * column, inverse)
            turn_cos, turn_sin = circle(quarter, wave * float(LANE), inverse)
            for tile in range(TILES):
                basis, at = (near, tile) if tile < KEPT else (far, tile - KEPT)
                basis[at, index, pl.ds(first, STEP), :] = cosine.astype(bf16)
                basis[at, index, pl.ds(PAIRS + first, STEP), :] = sine.astype(bf16)
                cosine, sine = cosine * turn_cos - sine * turn_sin, sine * turn_cos + cosine * turn_sin
            return carry

        lax.fori_loop(0, PAIRS // STEP, rows_of, 0)
        for tile in range(TILES - KEPT):
            at = large.at[index * (TILES - KEPT) + tile]
            outs.append(pltpu.make_async_copy(far.at[tile, index], far_hbm.at[tile, index], at))
            outs[-1].start()
    for copy in outs:
        copy.wait()


def fourier_kernel(
    me_ref, lat_owner_hbm, lat_points_hbm, received_ref, scale, near, far_hbm, out_hbm,
    lat_owner, lat_points, far, wide, narrow, left, ahead, back, grid, rounded, small, large,
):
    copies = [
        pltpu.make_async_copy(lat_owner_hbm, lat_owner, small.at[0]),
        pltpu.make_async_copy(lat_points_hbm, lat_points, small.at[1]),
    ]
    pieces = [pltpu.make_async_copy(far_hbm.at[tile], far.at[tile], large.at[tile]) for tile in range(TILES - KEPT)]
    for copy in copies + pieces:
        copy.start()
    grid[...] = jnp.zeros(grid.shape, f32)
    for source in range(N_WAVE):
        for part in range(SLOTS // 4):
            wide[pl.ds(source * 24 + 4 * part, 4), :] = received_ref[source, part].astype(f32)
    for index in range(2):
        for pair in range(PAIRS_DEV):
            slot = index * PAIRS_DEV + pair
            rows = wide[pl.ds(2 * pair + index, N_WAVE, stride=24), :]
            narrow[slot * N_WAVE : (slot + 1) * N_WAVE, :] = rows.astype(bf16)
    out_row, in_col = iota((COLS, COLS), 0), iota((COLS, COLS), 1)
    turn = jnp.where(in_col == 2 * (out_row % LEVELS) + out_row // LEVELS, 1.0, 0.0).astype(bf16)
    for index in range(2):
        turned = lax.dot_general(
            turn,
            narrow[index * PAIRS : (index + 1) * PAIRS, :],
            (((1,), (1,)), ((), ())),
            preferred_element_type=f32,
        )
        weighted = turned * scale[2 * index : 2 * index + 1, :]
        signed = turned * scale[2 * index + 1 : 2 * index + 2, :]
        left[index, 0, :LEVELS] = weighted[:LEVELS].astype(bf16)
        left[index, 1, :LEVELS] = weighted[LEVELS:].astype(bf16)
        if index == 0:
            left[index, 0, LEVELS:] = signed[:LEVELS].astype(bf16)
            left[index, 1, LEVELS:] = signed[LEVELS:].astype(bf16)
        else:
            left[index, 0, LEVELS:] = signed[LEVELS:].astype(bf16)
            left[index, 1, LEVELS:] = -signed[:LEVELS].astype(bf16)
    for copy in copies:
        copy.wait()
    quarter = my_points(me_ref, lat_owner, lat_points) // 4
    half = quarter // 2
    for first in range(0, EIGHTH, 2 * LANE):
        at = slice(first, first + 2 * LANE)
        tiles = range(first // LANE, first // LANE + 2)
        if tiles.start == KEPT:
            for piece in pieces:
                piece.wait()
        sums = []
        for index in range(2):
            right = jnp.concatenate(
                [near[tile, index] if tile < KEPT else far[tile - KEPT, index] for tile in tiles], axis=1
            )
            sums.append(jnp.dot(left[index, 0], right[:PAIRS], preferred_element_type=f32))
            sums.append(jnp.dot(left[index, 1], right[PAIRS:], preferred_element_type=f32))
        even_cos, even_sin, odd_cos, odd_sin = sums
        even, odd = even_cos + even_sin, odd_cos + odd_sin
        ahead[0, :, at] = even[:LEVELS] + odd[:LEVELS]
        ahead[1, :, at] = even[LEVELS:] - odd[LEVELS:]
        ahead[2, :, at] = even[:LEVELS] - odd[:LEVELS]
        ahead[3, :, at] = even[LEVELS:] + odd[LEVELS:]
        even, odd = even_cos - even_sin, odd_cos - odd_sin
        back[0, :, at] = even[LEVELS:] - odd[LEVELS:]
        back[1, :, at] = even[:LEVELS] - odd[:LEVELS]
        back[2, :, at] = even[LEVELS:] + odd[LEVELS:]
        back[3, :, at] = even[:LEVELS] + odd[:LEVELS]
    lane = iota((GROUP, LANE), 1)
    zero = jnp.zeros((GROUP, LANE), f32)
    outs = []
    for group in range(LEVELS // GROUP):
        rows = slice(group * GROUP, (group + 1) * GROUP)

        def put(tile, value, first, last):
            at = pl.ds(pl.multiple_of((tile + MARGIN) * LANE, LANE), LANE)
            point = lane + tile * LANE
            pltpu.store(grid.at[rows, at], value, mask=(point >= first) & (point <= last))

        for index in range(4):
            offset = index * quarter
            shift = offset % LANE
            before = zero
            for tile in range(TILES + (1 if index else 0)):
                now = zero
                if tile < TILES:
                    now = ahead[index, rows, tile * LANE : (tile + 1) * LANE]
                    if index:
                        now = pltpu.roll(now, shift, 1)
                value = jnp.where(lane < shift, before, now) if index else now
                put(offset // LANE + tile, value, offset, offset + half)
                before = now
            offset = (index + 1) * quarter
            shift = offset % LANE
            order = lax.rem(shift - lane + LANE, LANE)
            before = zero
            for tile in range(TILES + 1):
                now = zero
                if tile < TILES:
                    now = jnp.take_along_axis(
                        back[index, rows, tile * LANE : (tile + 1) * LANE], order, axis=1, mode="promise_in_bounds"
                    )
                value = jnp.where(lane <= shift, now, before)
                put(offset // LANE - tile, value, index * quarter + half + 1, offset - 1)
                before = now
        rounded[rows, :] = grid[rows, MARGIN * LANE :].astype(bf16)
        at = pl.ds(group * GROUP, GROUP)
        outs.append(pltpu.make_async_copy(rounded.at[at], out_hbm.at[0, at], small.at[2 + group]))
        outs[-1].start()
    for copy in outs:
        copy.wait()


def params(mib):
    return pltpu.CompilerParams(vmem_limit_bytes=mib * 1024 * 1024)


def per_device(spectral, table, wave_owner, lat_owner, lat_points):
    me = lax.axis_index("wave").astype(jnp.int32).reshape(1)
    waves = wave_owner.shape[0]
    tables = lax.all_gather(table, "lev", axis=0, tiled=False)
    spectral, wave_owner, lat_owner, lat_points = [
        pltpu.with_memory_space_constraint(array, pltpu.HBM)
        for array in (spectral, wave_owner, lat_owner, lat_points)
    ]
    owner_scratch = pltpu.VMEM((waves,), jnp.int32)
    lat_owner_scratch = pltpu.SMEM((NLAT,), jnp.int32)
    lat_points_scratch = pltpu.SMEM((NORTH,), jnp.int32)
    dma = pltpu.SemaphoreType.DMA
    four = pl.pallas_call(
        legendre_kernel,
        out_shape=pltpu.HBM((N_WAVE, SLOTS // 4, 4, COLS), bf16),
        in_specs=[SMEM, HBM, HBM, VMEM, HBM],
        out_specs=HBM,
        scratch_shapes=[
            owner_scratch,
            lat_owner_scratch,
            pltpu.VMEM((NORTH, ROWS_PAD), f32),
            pltpu.VMEM((ROWS_DEV, COLS), bf16),
            pltpu.VMEM((SLOTS * NLAT, COLS), f32),
            pltpu.VMEM((SLOTS // 4, N_WAVE, 4, COLS), bf16),
            dma((2,)),
            dma((len(PIECES),)),
            dma((SLOTS // 4,)),
        ],
        compiler_params=params(24),
        name="legendre",
    )(me, wave_owner, lat_owner, tables, spectral)
    received = lax.all_to_all(four, "wave", split_axis=0, concat_axis=0, tiled=True)
    near_shape = (KEPT, 2, 2 * PAIRS, LANE)
    far_shape = (TILES - KEPT, 2, 2 * PAIRS, LANE)
    near, far, scale = pl.pallas_call(
        basis_kernel,
        out_shape=(pltpu.VMEM(near_shape, bf16), pltpu.HBM(far_shape, bf16), pltpu.VMEM((8, PAIRS), f32)),
        in_specs=[SMEM, HBM, HBM, HBM, HBM],
        out_specs=(VMEM, HBM, VMEM),
        scratch_shapes=[
            owner_scratch,
            lat_owner_scratch,
            lat_points_scratch,
            pltpu.VMEM((2 * PAIRS, LANE), f32),
            pltpu.VMEM(far_shape, bf16),
            dma((3,)),
            dma((2 * (TILES - KEPT),)),
        ],
        compiler_params=params(16),
        name="basis",
    )(me, wave_owner, lat_owner, lat_points, pltpu.with_memory_space_constraint(four, pltpu.HBM))
    return pl.pallas_call(
        fourier_kernel,
        out_shape=pltpu.HBM((1, LEVELS, NLON_PAD), bf16),
        in_specs=[SMEM, HBM, HBM, VMEM, VMEM, VMEM, HBM],
        out_specs=HBM,
        scratch_shapes=[
            lat_owner_scratch,
            lat_points_scratch,
            pltpu.VMEM(far_shape, bf16),
            pltpu.VMEM((N_WAVE * 24, COLS), f32),
            pltpu.VMEM((SLOTS * N_WAVE, COLS), bf16),
            pltpu.VMEM((2, 2, COLS, PAIRS), bf16),
            pltpu.VMEM((4, LEVELS, EIGHTH), f32),
            pltpu.VMEM((4, LEVELS, EIGHTH), f32),
            pltpu.VMEM((LEVELS, MARGIN * LANE + NLON_PAD), f32),
            pltpu.VMEM((LEVELS, NLON_PAD), bf16),
            dma((2 + LEVELS // GROUP,)),
            dma((TILES - KEPT,)),
        ],
        compiler_params=params(24),
        name="fourier",
    )(
        me,
        lat_owner,
        lat_points,
        received,
        pltpu.with_memory_space_constraint(scale, pltpu.VMEM),
        pltpu.with_memory_space_constraint(near, pltpu.VMEM),
        pltpu.with_memory_space_constraint(far, pltpu.HBM),
    )


def solution(mesh):
    in_specs = (P("wave", "lev"), P("lev", "wave"), P(), P(), P())
    out_specs = P("wave", "lev", None)
    return jax.shard_map(
        per_device, mesh=mesh, in_specs=in_specs, out_specs=out_specs, check_vma=False
    )
```
